256 devices in a mesh: wave: 16 (over x, y), lev: 16 (over z, core).
Axes of the slice: x: 4, y: 4, z: 8, core: 2. Of those that a mesh axis runs over, the one named last changes fastest.
Arguments:
- spectral: bfloat16 [6, 128, 1296, 640], P(None, 'lev', 'wave'), may hold values from -0.119628906 to 0.119628906
- legendre: bfloat16 [640, 1296, 32], P('wave'), may hold values from -0.15625 to 0.15625
- pair_list: int32 [640], replicated, may hold values from 0 to 639, each once
- lon_counts: int32 [32], replicated, may hold values from 20 to 5136, as said below
- lat_order: int32 [32], replicated, may hold values from 0 to 31, each once
- layer_depth_log: float32 [128], P('lev'), may hold values from 0.04 to 0.2
- diagonal_layer_factor: float32 [128], P('lev'), may hold values from 0.02 to 0.12
Outputs:
- vorticity_grid: float32 [32, 128, 5376], P('wave', 'lev')
- divergence_grid: float32 [32, 128, 5376], P('wave', 'lev')
- temperature_grid: float32 [32, 128, 5376], P('wave', 'lev')
- temperature_slope: float32 [32, 128, 5376], P('wave', 'lev')
- height_energy: float32 [32, 128, 5376], P('wave', 'lev')
The draws below stay inside these ranges and needn't reach their ends.
Inputs may be any that keep to these rules, and one draw needn't show every extreme that they name: `pair_list`: a permutation; storage column s of spectral and legendre holds the wavenumbers pair_list[s] and 1279 - pair_list[s]. `lon_counts`: each value is 20 + 4 j for distinct j from 0 to 1279; the largest circle is always in the window. `lat_order`: A permutation.
All inputs are finite; a program needn't handle non-finite values.
Results may differ from the reference program's by a relative error of at most 0.0003.
Values may be sent and summed in bfloat16 or wider, within the bound.
A program may use at most 192 MiB of HBM per device.

```python
import math
import jax
import jax.numpy as jnp
from jax import lax

TRUNC = 1279
PAIRS = 640
ROWS = 1281
ROWS_PAD = 1296
LON_PAD = 5376
LEVELS = 128
LATS = 32


def draw_lon_counts(key, part):
    first_key, second_key = jax.random.split(jax.random.fold_in(key, 11))
    picks = jax.random.permutation(first_key, TRUNC)[:LATS]
    position = jax.random.randint(second_key, (), 0, LATS)
    picks = picks.at[position].set(TRUNC)
    return (20 + 4 * picks).astype(jnp.int32)


def steps_of(stream_key, extent, cuts, low, high):
    def one(dim, shards_of):
        steps = jax.random.uniform(jax.random.fold_in(jax.random.fold_in(stream_key, 6), dim), (shards_of,), jnp.float32, low / len(cuts), high / len(cuts))
        return jnp.repeat(jnp.exp(steps), extent[dim] // shards_of).reshape((-1,) + (1,) * (len(extent) - dim - 1))

    gain = one(*cuts[0])
    for cut in cuts[1:]:
        gain = gain * one(*cut)
    return gain


def gaussian(key, extent, deviation, most, shards=(), kind=jnp.bfloat16):
    level = steps_of(key, extent, shards, -0.22, 0.18) if shards else 1.0
    array = jax.random.normal(key, extent, jnp.float32) * deviation * level
    return jnp.minimum(jnp.maximum(array, -most), most).astype(kind)


def setup_inputs(seed: int = 0) -> dict:
    streams_of = jax.random.split(jax.random.key(seed), 8)
    return {
        "spectral": gaussian(streams_of[0], (6, LEVELS, ROWS_PAD, PAIRS), 0.02, 0.119628906, ((1, 16), (2, 16))),
        "legendre": gaussian(streams_of[1], (PAIRS, ROWS_PAD, LATS), ROWS ** -0.5, 0.15625, ((0, 16),)),
        "pair_list": jax.random.permutation(streams_of[2], PAIRS).astype(jnp.int32),
        "lon_counts": draw_lon_counts(jax.random.fold_in(streams_of[7], 71), 0),
        "lat_order": jax.random.permutation(streams_of[4], LATS).astype(jnp.int32),
        "layer_depth_log": jnp.clip(jnp.exp(math.log(0.2) - 1.609438 * jax.random.uniform(streams_of[5], (LEVELS,), jnp.float32) ** steps_of(streams_of[5], (LEVELS,), ((0, 16),), -0.2, 0.2)), 0.04, 0.2),
        "diagonal_layer_factor": jnp.clip(jnp.exp(math.log(0.12) - 1.7917595 * jax.random.uniform(streams_of[6], (LEVELS,), jnp.float32) ** steps_of(streams_of[6], (LEVELS,), ((0, 16),), -0.2, 0.2)), 0.02, 0.12),
    }


def legendre_split(spec_rows, polynomials, pair_ids, row_start):
    row_index = row_start + lax.broadcasted_iota(jnp.int32, (spec_rows.shape[2], spec_rows.shape[3]), 0)
    boundary = TRUNC + 1 - pair_ids[None, :]
    low_mask = row_index < boundary
    high_mask = (row_index >= boundary) & (row_index < ROWS)
    zero_value = jnp.zeros((), spec_rows.dtype)
    first_part = jnp.where(low_mask, spec_rows, zero_value)
    second_part = jnp.where(high_mask, spec_rows, zero_value)
    stacked = jnp.stack([first_part, second_part], 0)
    return jnp.einsum("hclrp,prq->qhclp", stacked, polynomials, preferred_element_type=jnp.float32)


def synthesis_basis(wavenumbers, lon_totals, first_column, block_width):
    columns = first_column + lax.broadcasted_iota(jnp.int32, (1, 1, block_width), 2)
    wave_grid = wavenumbers[None, :, None]
    circle = lon_totals[:, None, None]
    phases = (wave_grid * columns) % circle
    angles = phases.astype(jnp.float32) / circle.astype(jnp.float32) * (2.0 * jnp.pi)
    kept_mask = (2 * wave_grid < circle) & (columns < circle)
    weights = jnp.where(kept_mask, jnp.where(wave_grid == 0, 1.0, 2.0), 0.0).astype(jnp.float32)
    return jnp.concatenate([weights * jnp.cos(angles), weights * jnp.sin(angles)], axis=1)


def synthesis_rows(harmonic_amplitude, wavenumbers):
    factors = wavenumbers.astype(jnp.float32) / (TRUNC + 1)
    rotation_rate_values = jnp.concatenate([harmonic_amplitude[..., 0, :, :], -harmonic_amplitude[..., 1, :, :]], -1)
    spreading_rate_values = jnp.concatenate([harmonic_amplitude[..., 2, :, :], -harmonic_amplitude[..., 3, :, :]], -1)
    thermal_state_values = jnp.concatenate([harmonic_amplitude[..., 4, :, :], -harmonic_amplitude[..., 5, :, :]], -1)
    zonal_slope_values = jnp.concatenate([-factors * harmonic_amplitude[..., 5, :, :], -factors * harmonic_amplitude[..., 4, :, :]], -1)
    return jnp.stack([rotation_rate_values, spreading_rate_values, thermal_state_values, zonal_slope_values], -3)


def reference(spectral, legendre, pair_list, lon_counts, lat_order, layer_depth_log, diagonal_layer_factor):
    polynomials = legendre.astype(jnp.float32)

    def per_level(spec_level):
        values = legendre_split(spec_level[:, None].astype(jnp.float32), polynomials, pair_list, 0)
        return values[:, :, :, 0, :]

    fourier = lax.map(per_level, jnp.moveaxis(spectral, 1, 0))
    wavenumbers = jnp.concatenate([pair_list, TRUNC - pair_list])

    def per_row(slot_index):
        latitude = lat_order[slot_index]
        lon_total = lax.dynamic_index_in_dim(lon_counts, latitude, 0, keepdims=True)
        harmonic_amplitude = lax.dynamic_index_in_dim(fourier, latitude, 1, keepdims=False)
        harmonic_amplitude = jnp.transpose(harmonic_amplitude, (2, 0, 1, 3)).reshape(6, LEVELS, 2 * PAIRS)
        left_rows = synthesis_rows(harmonic_amplitude, wavenumbers).reshape(4 * LEVELS, 4 * PAIRS)
        basis_full = synthesis_basis(wavenumbers, lon_total, 0, LON_PAD)[0]
        product = jnp.dot(left_rows, basis_full, precision=lax.Precision.HIGHEST, preferred_element_type=jnp.float32)
        return product.reshape(4, LEVELS, LON_PAD)

    physical_space_lines = lax.map(per_row, jnp.arange(LATS, dtype=jnp.int32))
    thermal_state_values = physical_space_lines[:, 2]
    scaled_contributions = layer_depth_log[None, :, None] * thermal_state_values
    beneath_layers_total = jnp.flip(jnp.cumsum(jnp.flip(scaled_contributions, 1), 1), 1) - scaled_contributions
    height_energy = diagonal_layer_factor[None, :, None] * thermal_state_values + beneath_layers_total
    return physical_space_lines[:, 0], physical_space_lines[:, 1], thermal_state_values, physical_space_lines[:, 3], height_energy
```

```python
import functools

import jax
import jax.numpy as jnp
from jax import lax
from jax.experimental import pallas as pl
from jax.experimental.pallas import tpu as pltpu
from jax.sharding import PartitionSpec as P

TRUNC = 1279
ROWS = 1281
LON_PAD = 5376
WAVES = 1280
STRIP = 768
STRIPS = LON_PAD // STRIP

COS_TERMS = (1.0, -19.73920440673828, 64.93911743164062, -85.45011138916016,
             60.16740036010742, -25.966703414916992, 6.5273566246032715)
SIN_TERMS = (6.2831854820251465, -41.34170150756836, 81.60513305664062, -76.7030029296875,
             42.02582931518555, -14.899463653564453, 3.2375807762145996)


def turn(product, circle):
    inverse = 1.0 / circle
    part = (product - jnp.floor(product * inverse + 0.5) * circle) * inverse
    square = part * part
    cosine = jnp.full_like(square, COS_TERMS[-1])
    sine = jnp.full_like(square, SIN_TERMS[-1])
    for term in COS_TERMS[-2::-1]:
        cosine = cosine * square + term
    for term in SIN_TERMS[-2::-1]:
        sine = sine * square + term
    return cosine, sine * part


def halves(value):
    high = value.astype(jnp.bfloat16)
    return high, (value - high.astype(jnp.float32)).astype(jnp.bfloat16)


def synthesis_kernel(counts, coef, waves_row, waves_column, entering, mixing,
                     out_v, out_d, out_t, out_s, out_h,
                     basis_high, basis_low, left_high, left_low, twist):
    circle_whole = counts[pl.program_id(0)]
    circle = jnp.full((1, 1), circle_whole, jnp.int32).astype(jnp.float32)

    def basis_rows(block, _):
        rows = pl.ds(pl.multiple_of(block * 16, 16), 16)
        other = pl.ds(pl.multiple_of(block * 16 + WAVES, 16), 16)
        column = lax.broadcasted_iota(jnp.int32, (16, STRIP), 1).astype(jnp.float32)
        cosine, sine = turn(waves_column[rows, :1] * column, circle)
        basis_high[rows, :], basis_low[rows, :] = halves(cosine)
        basis_high[other, :], basis_low[other, :] = halves(sine)
        return 0

    lax.fori_loop(0, WAVES // 16, basis_rows, 0)

    wave = waves_row[...]
    weight = jnp.where(2.0 * wave < circle, jnp.where(wave == 0.0, 1.0, 2.0), 0.0)
    start = (lax.broadcasted_iota(jnp.int32, (8, WAVES), 0) * STRIP).astype(jnp.float32)
    cosine, sine = turn(start * wave, circle)
    twist[0] = cosine * weight
    twist[1] = sine * weight
    factor = wave * (1.0 / (TRUNC + 1))

    def rows_of(field):
        if field < 3:
            return coef[0, 2 * field], coef[0, 2 * field + 1]
        real, imaginary = coef[0, 4], coef[0, 5]
        if field == 3:
            return -factor * imaginary, factor * real
        upper = []
        for value, side in ((real, 0), (imaginary, 1)):
            total = jnp.broadcast_to(entering[0, side : side + 1, :], (8, WAVES))
            for level in range(8):
                total = total + mixing[:, level : level + 1] * value[level : level + 1, :]
            upper.append(total)
        return upper[0], upper[1]

    for field in range(5):
        real, imaginary = rows_of(field)
        for strip in range(STRIPS):
            at = strip * 40 + field * 8
            cosine = twist[0, strip : strip + 1, :]
            sine = twist[1, strip : strip + 1, :]
            high, low = halves(real * cosine - imaginary * sine)
            left_high[at : at + 8, :WAVES] = high
            left_low[at : at + 8, :WAVES] = low
            high, low = halves(-(real * sine + imaginary * cosine))
            left_high[at : at + 8, WAVES:] = high
            left_low[at : at + 8, WAVES:] = low

    def block_of(block, _):
        first = pl.multiple_of(block * 256, 256)
        columns = pl.ds(first, 256)
        times = functools.partial(jnp.dot, preferred_element_type=jnp.float32)
        high = basis_high[:, columns]
        result = (times(left_high[...], high) + times(left_low[...], high)
                  + times(left_high[...], basis_low[:, columns]))
        lane = lax.broadcasted_iota(jnp.int32, (40, 256), 1) + first
        for strip in range(STRIPS):
            piece = jnp.where(lane + strip * STRIP < circle_whole,
                              result[strip * 40 : strip * 40 + 40], 0.0)
            where = pl.ds(pl.multiple_of(first + strip * STRIP, 256), 256)
            for field, out in enumerate((out_v, out_d, out_t, out_s, out_h)):
                out[0, :, where] = piece[field * 8 : field * 8 + 8]
        return 0

    lax.fori_loop(0, STRIP // 256, block_of, 0)


def synthesize(counts, coef, waves, entering, mixing):
    lats = coef.shape[0]
    whole = pl.BlockSpec(memory_space=pltpu.VMEM)
    grid_line = pl.BlockSpec((1, 8, LON_PAD), lambda i: (i, 0, 0))
    return pl.pallas_call(
        synthesis_kernel,
        grid=(lats,),
        out_shape=[jax.ShapeDtypeStruct((lats, 8, LON_PAD), jnp.float32)] * 5,
        in_specs=[
            pl.BlockSpec(memory_space=pltpu.SMEM),
            pl.BlockSpec((1, 6, 8, WAVES), lambda i: (i, 0, 0, 0)),
            whole,
            whole,
            pl.BlockSpec((1, 2, WAVES), lambda i: (i, 0, 0)),
            whole,
        ],
        out_specs=[grid_line] * 5,
        scratch_shapes=[
            pltpu.VMEM((2 * WAVES, STRIP), jnp.bfloat16),
            pltpu.VMEM((2 * WAVES, STRIP), jnp.bfloat16),
            pltpu.VMEM((STRIPS * 40 + 8, 2 * WAVES), jnp.bfloat16),
            pltpu.VMEM((STRIPS * 40 + 8, 2 * WAVES), jnp.bfloat16),
            pltpu.VMEM((2, 8, WAVES), jnp.float32),
        ],
        compiler_params=pltpu.CompilerParams(vmem_limit_bytes=50 * 2**20),
    )(counts, coef, waves[None, :], jnp.broadcast_to(waves[:, None], (WAVES, 128)), entering, mixing)


def legendre_split(spec_rows, polynomials, pair_ids):
    row_index = lax.broadcasted_iota(jnp.int32, (spec_rows.shape[2], spec_rows.shape[3]), 0)
    boundary = TRUNC + 1 - pair_ids[None, :]
    low_mask = row_index < boundary
    high_mask = (row_index >= boundary) & (row_index < ROWS)
    zero_value = jnp.zeros((), spec_rows.dtype)
    first_part = jnp.where(low_mask, spec_rows, zero_value)
    second_part = jnp.where(high_mask, spec_rows, zero_value)
    stacked = jnp.stack([first_part, second_part], 0)
    return jnp.einsum("hclrp,prq->qhclp", stacked, polynomials, preferred_element_type=jnp.float32)


def body(
    spectral, legendre, pair_list, lon_counts, lat_order, layer_depth_log, diagonal_layer_factor
):
    group_count = lax.axis_size("wave")
    group_index = lax.axis_index("wave")
    pair_share = pair_list.shape[0] // group_count
    lat_share = lat_order.shape[0] // group_count
    own_pairs = lax.dynamic_slice_in_dim(pair_list, group_index * pair_share, pair_share)
    own_lats = lax.dynamic_slice_in_dim(lat_order, group_index * lat_share, lat_share)
    chosen = own_lats[:, None] == jnp.arange(lat_order.shape[0])[None, :]
    own_counts = jnp.sum(jnp.where(chosen, lon_counts[None, :], 0), axis=1)
    waves = jnp.concatenate([pair_list, TRUNC - pair_list]).astype(jnp.float32)

    slots = (jnp.arange(lat_order.shape[0])[:, None] == lat_order[None, :]).astype(jnp.bfloat16)
    polynomials = jnp.einsum(
        "prq,qi->pri", legendre, slots, preferred_element_type=jnp.float32
    ).astype(jnp.bfloat16)
    values = legendre_split(
        lax.all_to_all(spectral, "wave", split_axis=3, concat_axis=2, tiled=True),
        polynomials,
        own_pairs,
    )
    fourier = lax.all_to_all(values, "wave", split_axis=0, concat_axis=4, tiled=True)
    coef = jnp.transpose(fourier, (0, 2, 3, 1, 4)).reshape(lat_share, 6, 8, WAVES)

    scaled = jnp.sum(layer_depth_log[None, None, :, None] * coef[:, 4:], axis=2)
    pieces = lax.all_gather(scaled, "lev")
    later = jnp.arange(pieces.shape[0]) > lax.axis_index("lev")
    entering = jnp.sum(jnp.where(later[:, None, None, None], pieces, 0.0), axis=0)
    level = jnp.arange(8)
    mixing = jnp.where(
        level[None, :] == level[:, None],
        diagonal_layer_factor[:, None],
        jnp.where(level[None, :] > level[:, None], layer_depth_log[None, :], 0.0),
    )
    return tuple(synthesize(own_counts, coef, waves, entering, mixing))


def solution(mesh):
    placed = (
        P(None, "lev", "wave", None),
        P("wave", None, None),
        P(),
        P(),
        P(),
        P("lev"),
        P("lev"),
    )
    return jax.shard_map(
        body,
        mesh=mesh,
        in_specs=placed,
        out_specs=(P("wave", "lev", None),) * 5,
        check_vma=False,
    )
```

```python
import functools

import jax
import jax.numpy as jnp
from jax import lax
from jax.experimental import pallas as pl
from jax.experimental.pallas import tpu as pltpu
from jax.sharding import PartitionSpec as P

TRUNC = 1279
ROWS = 1281
LON_PAD = 5376
WAVES = 1280
STRIP = 768
STRIPS = LON_PAD // STRIP
PEERS = 16
SHARE = 40
HALVES = (320, 328)
ORDER = ((2, 2), (1, 0), (3, 0), (0, 1), (0, 3), (1, 2), (3, 2), (2, 1), (2, 3), (2, 0), (0, 2),
         (1, 1), (3, 3), (1, 3), (3, 1))
MESH = pl.DeviceIdType.MESH

COS_TERMS = (1.0, -19.73920440673828, 64.93911743164062, -85.45011138916016,
             60.16740036010742, -25.966703414916992, 6.5273566246032715)
SIN_TERMS = (6.2831854820251465, -41.34170150756836, 81.60513305664062, -76.7030029296875,
             42.02582931518555, -14.899463653564453, 3.2375807762145996)


def turn(product, circle):
    inverse = 1.0 / circle
    part = (product - jnp.floor(product * inverse + 0.5) * circle) * inverse
    square = part * part
    cosine = jnp.full_like(square, COS_TERMS[-1])
    sine = jnp.full_like(square, SIN_TERMS[-1])
    for term in COS_TERMS[-2::-1]:
        cosine = cosine * square + term
    for term in SIN_TERMS[-2::-1]:
        sine = sine * square + term
    return cosine, sine * part


def halves(value):
    high = value.astype(jnp.bfloat16)
    return high, (value - high.astype(jnp.float32)).astype(jnp.bfloat16)


def exchange_kernel(pairs, lon_counts, lat_order, depth, spectral, legendre, pair_row, slots,
                    out_fourier, out_above, out_basis,
                    spec, legs, send_a, send_b, got_a, got_b, stage, rights, lefts, shuffle,
                    summed, send_f, got_f, send_c, got_c, column, table,
                    in_sem, leg_sem, spec_send, spec_recv, spec_own, four_send, four_recv, four_own,
                    lev_send, lev_recv, table_sem):
    wave, lev = lax.axis_index("wave"), lax.axis_index("lev")
    across, along = wave // 4, lax.rem(wave, 4)
    times = functools.partial(jnp.dot, preferred_element_type=jnp.float32)

    loads = []
    for part in (1, 0):
        load = pltpu.make_async_copy(spectral.at[pl.ds(3 * part, 3)], spec.at[pl.ds(3 * part, 3)],
                                     in_sem.at[part])
        load.start()
        loads.append(load)
    leg_load = pltpu.make_async_copy(legendre, legs, leg_sem)
    leg_load.start()

    barrier = pltpu.get_barrier_semaphore()
    for step in range(1, PEERS):
        pl.semaphore_signal(barrier, inc=1, device_id=(lax.rem(wave + step, PEERS), lev),
                            device_id_type=MESH)
        pl.semaphore_signal(barrier, inc=1, device_id=(wave, lax.rem(lev + step, PEERS)),
                            device_id_type=MESH)

    def window(duo):
        return jnp.minimum((80 * duo) // 128, 3) * 128

    def shuffle_rows(duo, _):
        lane = lax.broadcasted_iota(jnp.int32, (1, 256), 1)
        second = jnp.where(lane >= 128, 1, 0)
        inner = lane - 128 * second
        third = jnp.where(inner >= 40, 1, 0) + jnp.where(inner >= 80, 1, 0) + jnp.where(inner >= 120, 1, 0)
        source = 80 * duo - window(duo) + 40 * second + inner - 40 * third
        row = lax.broadcasted_iota(jnp.int32, (256, 256), 0)
        for place in range(3):
            wanted = jnp.where(third == place, source, -1)
            shuffle[duo, place] = jnp.where(row == wanted, 1.0, 0.0).astype(jnp.bfloat16)
        return 0

    lax.fori_loop(0, 8, shuffle_rows, 0)
    pl.semaphore_wait(barrier, 2 * (PEERS - 1))

    copies = []
    waits = {}
    for part in (1, 0):
        loads[1 - part].wait()
        for half, (rows, send, got) in enumerate(zip(HALVES, (send_a, send_b), (got_a, got_b))):
            first = half * HALVES[0]

            def shuffled(duo, _, part=part, first=first, rows=rows, send=send):
                lanes = pl.ds(pl.multiple_of(window(duo), 128), 256)
                total = times(spec[3 * part, first : first + rows, lanes], shuffle[duo, 0])
                for place in (1, 2):
                    total = total + times(spec[3 * part + place, first : first + rows, lanes],
                                          shuffle[duo, place])
                send[part, 2 * duo] = total[:, :128].astype(jnp.bfloat16)
                send[part, 2 * duo + 1] = total[:, 128:].astype(jnp.bfloat16)
                return 0

            lax.fori_loop(0, 8, shuffled, 0)
            here = []
            for number, (x, y) in enumerate(ORDER):
                other = lax.rem(across + x, 4) * 4 + lax.rem(along + y, 4)
                copy = pltpu.make_async_remote_copy(
                    src_ref=send.at[part, other], dst_ref=got.at[part, wave],
                    send_sem=spec_send.at[part, half, number], recv_sem=spec_recv.at[part, half, number],
                    device_id=(other, lev), device_id_type=MESH)
                copy.start()
                here.append(copy)
            own = pltpu.make_async_copy(send.at[part, wave], got.at[part, wave], spec_own.at[part, half])
            own.start()
            waits[part, half] = (here, own)
            copies += here

    leg_load.wait()

    def masked(place, _):
        boundary = TRUNC + 1 - pairs[wave * SHARE + place]
        values = legs[place].astype(jnp.float32)
        row = lax.broadcasted_iota(jnp.int32, values.shape, 1)
        low = jnp.where(row < boundary, values, 0.0)
        high = jnp.where((row >= boundary) & (row < ROWS), values, 0.0)
        lefts[pl.ds(pl.multiple_of(place * 64, 64), 32), :] = low.astype(jnp.bfloat16)
        lefts[pl.ds(pl.multiple_of(place * 64 + 32, 32), 32), :] = high.astype(jnp.bfloat16)
        return 0

    lax.fori_loop(0, SHARE, masked, 0)
    column[...] = jnp.transpose(jnp.broadcast_to(pair_row[...].astype(jnp.float32), (128, 640)))

    def table_copy(lat, block):
        slot = lax.rem(block, 2)
        return pltpu.make_async_copy(
            table.at[slot], out_basis.at[lat, :, :, pl.ds(pl.multiple_of(block * 128, 128), 128), :],
            table_sem.at[slot])

    def tables(lat):
        whole = lon_counts[lat_order[2 * wave + lat]]
        circle = jnp.full((1, 1), whole, jnp.int32).astype(jnp.float32)

        def block_of(block, _):
            slot = lax.rem(block, 2)

            @pl.when(block >= 2)
            def _():
                table_copy(lat, block - 2).wait()

            low = block < 5
            at = (block - jnp.where(low, 0, 5)) * 128
            base = jnp.where(low, 0.0, float(TRUNC))
            sign = jnp.where(low, 1.0, -1.0)

            def rows_of(step, _):
                rows = pl.ds(pl.multiple_of(step * 16, 16), 16)
                strip = lax.broadcasted_iota(jnp.int32, (16, STRIP), 1).astype(jnp.float32)
                source = column[pl.ds(pl.multiple_of(at + step * 16, 16), 16), :]
                number = jnp.concatenate([base + sign * source] * (STRIP // 128), axis=1)
                cosine, sine = turn(number * strip, circle)
                table[slot, 0, 0, rows, :], table[slot, 1, 0, rows, :] = halves(cosine)
                table[slot, 0, 1, rows, :], table[slot, 1, 1, rows, :] = halves(sine)
                return 0

            lax.fori_loop(0, 8, rows_of, 0)
            table_copy(lat, block).start()
            return 0

        lax.fori_loop(0, 10, block_of, 0)
        table_copy(lat, 8).wait()
        table_copy(lat, 9).wait()

    def legendre_sums(part):
        for half in (0, 1):
            here, own = waits[part, half]
            for copy in here:
                copy.wait_recv()
            own.wait()

        def widen(source, _):
            stage[pl.ds(pl.multiple_of(source * 648, 8), 320), :] = got_a[part, source].astype(jnp.float32)
            stage[pl.ds(pl.multiple_of(source * 648 + 320, 8), 328), :] = got_b[part, source].astype(jnp.float32)
            return 0

        lax.fori_loop(0, PEERS, widen, 0)

        def gather(chunk, _):
            rows = pl.ds(pl.multiple_of(chunk * 144, 16), 144)
            for level in range(8):
                taken = stage[pl.ds(chunk * 1152 + level, 144, stride=8), :]
                lanes = slice(128 * (level % 2), 128 * (level % 2) + 128)
                rights[level // 2, rows, lanes] = taken.astype(jnp.bfloat16)
            return 0

        lax.fori_loop(0, 9, gather, 0)
        lane = lax.broadcasted_iota(jnp.int32, (1, 256), 1)
        inner = jnp.where(lane >= 128, lane - 128, lane)
        inner = jnp.where(inner >= 80, inner - 80, jnp.where(inner >= 40, inner - 40, inner))

        def levels(duo, _):
            def group(chunk, total):
                result = times(lefts[pl.ds(pl.multiple_of(chunk * 512, 512), 512), :], rights[duo])
                for place in range(8):
                    total = total + jnp.where(inner == chunk * 8 + place,
                                              result[place * 64 : place * 64 + 64], 0.0)
                return total

            summed[duo] = lax.fori_loop(0, 5, group, jnp.zeros((64, 256), jnp.float32))
            return 0

        lax.fori_loop(0, 4, levels, 0)
        for duo in range(4):
            rest = summed[duo]
            moved = jnp.zeros((64, 256), jnp.float32)
            for _ in range(3):
                piece = rest.astype(jnp.bfloat16)
                rest = rest - piece.astype(jnp.float32)
                moved = moved + times(slots[...], piece)
            send_f[part, pl.ds(2 * duo, 64, stride=8), :] = moved[:, :128]
            send_f[part, pl.ds(2 * duo + 1, 64, stride=8), :] = moved[:, 128:]
        here = []
        for number, (x, y) in enumerate(ORDER):
            other = lax.rem(across + x, 4) * 4 + lax.rem(along + y, 4)
            copy = pltpu.make_async_remote_copy(
                src_ref=send_f.at[part, pl.ds(pl.multiple_of(other * 32, 32), 32), :],
                dst_ref=got_f.at[part, pl.ds(pl.multiple_of(wave * 32, 32), 32), :],
                send_sem=four_send.at[part, number], recv_sem=four_recv.at[part, number],
                device_id=(other, lev), device_id_type=MESH)
            copy.start()
            here.append(copy)
        own = pltpu.make_async_copy(
            send_f.at[part, pl.ds(pl.multiple_of(wave * 32, 32), 32), :],
            got_f.at[part, pl.ds(pl.multiple_of(wave * 32, 32), 32), :], four_own.at[part])
        own.start()
        copies.extend(here)
        return here, own

    def arrived(here, own):
        for copy in here:
            copy.wait_recv()
        own.wait()

    tables(0)
    tables(1)
    first = legendre_sums(1)
    arrived(*first)
    level = lax.broadcasted_iota(jnp.int32, (1, 8, 128), 1)
    share = jnp.zeros((1, 8, 128), jnp.float32)
    for number in range(8):
        share = jnp.where(level == number, depth[number], share)
    send_c[...] = jnp.sum(got_f[1].reshape(64, 8, 128) * share, axis=1)
    lev_copies = []
    for step in range(1, PEERS):
        copy = pltpu.make_async_remote_copy(
            src_ref=send_c, dst_ref=got_c.at[lev],
            send_sem=lev_send.at[step - 1], recv_sem=lev_recv.at[step - 1],
            device_id=(wave, lax.rem(lev + step, PEERS)), device_id_type=MESH)
        copy.start()
        lev_copies.append(copy)
    out_fourier[1] = got_f[1]
    second = legendre_sums(0)
    for copy in lev_copies:
        copy.wait_recv()
    above = jnp.zeros((64, 128), jnp.float32)
    got_c[lev] = send_c[...]
    for other in range(PEERS):
        above = above + jnp.where(other > lev, got_c[other], 0.0)
    out_above[...] = above
    arrived(*second)
    out_fourier[0] = got_f[0]
    for copy in copies + lev_copies:
        copy.wait_send()


def exchange(pairs, lon_counts, lat_order, depth, spectral, legendre, pair_row, slots):
    anywhere = pl.BlockSpec(memory_space=pl.ANY)
    vector = pl.BlockSpec(memory_space=pltpu.VMEM)
    scalar = pl.BlockSpec(memory_space=pltpu.SMEM)
    dma = pltpu.SemaphoreType.DMA
    return pl.pallas_call(
        exchange_kernel,
        out_shape=[
            jax.ShapeDtypeStruct((2, 512, 128), jnp.float32),
            jax.ShapeDtypeStruct((64, 128), jnp.float32),
            jax.ShapeDtypeStruct((2, 2, 2, WAVES, STRIP), jnp.bfloat16),
        ],
        in_specs=[scalar] * 4 + [anywhere] * 2 + [vector] * 2,
        out_specs=[vector, vector, anywhere],
        scratch_shapes=[
            pltpu.VMEM((6, 648, 640), jnp.bfloat16),
            pltpu.VMEM((SHARE, 32, 1296), jnp.bfloat16),
            pltpu.VMEM((2, PEERS, HALVES[0], 128), jnp.bfloat16),
            pltpu.VMEM((2, PEERS, HALVES[1], 128), jnp.bfloat16),
            pltpu.VMEM((2, PEERS, HALVES[0], 128), jnp.bfloat16),
            pltpu.VMEM((2, PEERS, HALVES[1], 128), jnp.bfloat16),
            pltpu.VMEM((PEERS * 648, 128), jnp.float32),
            pltpu.VMEM((4, 1296, 256), jnp.bfloat16),
            pltpu.VMEM((SHARE * 64, 1296), jnp.bfloat16),
            pltpu.VMEM((8, 3, 256, 256), jnp.bfloat16),
            pltpu.VMEM((4, 64, 256), jnp.float32),
            pltpu.VMEM((2, 512, 128), jnp.float32),
            pltpu.VMEM((2, 512, 128), jnp.float32),
            pltpu.VMEM((64, 128), jnp.float32),
            pltpu.VMEM((PEERS, 64, 128), jnp.float32),
            pltpu.VMEM((640, 128), jnp.float32),
            pltpu.VMEM((2, 2, 2, 128, STRIP), jnp.bfloat16),
            dma((2,)), dma, dma((2, 2, 15)), dma((2, 2, 15)), dma((2, 2)),
            dma((2, 15)), dma((2, 15)), dma((2,)), dma((15,)), dma((15,)), dma((2,)),
        ],
        compiler_params=pltpu.CompilerParams(
            collective_id=0, has_side_effects=True, vmem_limit_bytes=56 * 2**20
        ),
    )(pairs, lon_counts, lat_order, depth, spectral, legendre, pair_row, slots)


def synthesis_kernel(lon_counts, lat_order, depth, diagonal, fourier, above, pair_row, basis,
                     out_v, out_d, out_t, out_s, out_h,
                     table, left_high, left_low, twist, coef, upper, table_sem):
    lat = pl.program_id(0)
    wave_group = lax.axis_index("wave")

    def load(which):
        return pltpu.make_async_copy(basis.at[which], table.at[which], table_sem.at[which])

    @pl.when(lat == 0)
    def _():
        load(0).start()
        load(1).start()

    circle_whole = lon_counts[lat_order[2 * wave_group + lat]]
    circle = jnp.full((1, 1), circle_whole, jnp.int32).astype(jnp.float32)
    lane = lax.broadcasted_iota(jnp.int32, (1, 128), 1)

    def spread(take, keep, height):
        for place in range(3):
            tiles = [jnp.zeros((height, 128), jnp.float32)] * 5
            for source in range(PEERS):
                value = take(source)
                goal = source * SHARE
                tile, offset = goal // 128, goal % 128
                rolled = pltpu.roll(value, (offset - place * SHARE) % 128, 1)
                end = offset + SHARE
                tiles[tile] = jnp.where((lane >= offset) & (lane < end), rolled, tiles[tile])
                if end > 128:
                    tiles[tile + 1] = jnp.where(lane < end - 128, rolled, tiles[tile + 1])
            for tile in range(5):
                keep(place, tile, tiles[tile])

    for part in range(2):
        for side in range(2):
            def take(source, part=part, side=side):
                return fourier[part, pl.ds(pl.multiple_of(source * 32 + lat * 16 + side * 8, 8), 8), :]

            def keep(place, tile, value, part=part, side=side):
                at = side * 640 + tile * 128
                coef[3 * part + place, :, at : at + 128] = value

            spread(take, keep, 8)

    def take_above(source):
        return above[source]

    def keep_above(place, tile, value):
        upper[place, :, tile * 128 : tile * 128 + 128] = value

    spread(take_above, keep_above, 4)

    pair = pair_row[...].astype(jnp.float32)
    wave = jnp.concatenate([pair, TRUNC - pair], axis=1)
    weight = jnp.where(2.0 * wave < circle, jnp.where(wave == 0.0, 1.0, 2.0), 0.0)
    start = (lax.broadcasted_iota(jnp.int32, (8, WAVES), 0) * STRIP).astype(jnp.float32)
    cosine, sine = turn(start * wave, circle)
    twist[0] = cosine * weight
    twist[1] = sine * weight
    factor = wave * (1.0 / (TRUNC + 1))
    level_of = lax.broadcasted_iota(jnp.int32, (8, 1), 0)

    def rows_of(field):
        if field < 3:
            return coef[2 * field], coef[2 * field + 1]
        real, imaginary = coef[4], coef[5]
        if field == 3:
            return -factor * imaginary, factor * real
        higher = []
        for value, place in ((real, 1), (imaginary, 2)):
            total = jnp.broadcast_to(
                jnp.concatenate([upper[place, pl.ds(2 * lat, 1), :], upper[place, pl.ds(2 * lat + 1, 1), :]], axis=1),
                (8, WAVES))
            for level in range(8):
                share = jnp.where(level_of == level, diagonal[level],
                                  jnp.where(level_of < level, depth[level], 0.0))
                total = total + share * value[level : level + 1, :]
            higher.append(total)
        return higher[0], higher[1]

    for field in range(5):
        real, imaginary = rows_of(field)
        for strip in range(STRIPS):
            at = strip * 40 + field * 8
            cosine = twist[0, strip : strip + 1, :]
            sine = twist[1, strip : strip + 1, :]
            high, low = halves(real * cosine - imaginary * sine)
            left_high[0, at : at + 8, :] = high
            left_low[0, at : at + 8, :] = low
            high, low = halves(-(real * sine + imaginary * cosine))
            left_high[1, at : at + 8, :] = high
            left_low[1, at : at + 8, :] = low

    load(lat).wait()

    def block_of(block, _):
        first = pl.multiple_of(block * 256, 256)
        columns = pl.ds(first, 256)
        times = functools.partial(jnp.dot, preferred_element_type=jnp.float32)
        result = None
        for trig in (0, 1):
            high = table[lat, 0, trig, :, columns]
            term = (times(left_high[trig], high) + times(left_low[trig], high)
                    + times(left_high[trig], table[lat, 1, trig, :, columns]))
            result = term if result is None else result + term
        number = lax.broadcasted_iota(jnp.int32, (40, 256), 1) + first
        for strip in range(STRIPS):
            piece = jnp.where(number + strip * STRIP < circle_whole,
                              result[strip * 40 : strip * 40 + 40], 0.0)
            where = pl.ds(pl.multiple_of(first + strip * STRIP, 256), 256)
            for field, out in enumerate((out_v, out_d, out_t, out_s, out_h)):
                out[0, :, where] = piece[field * 8 : field * 8 + 8]
        return 0

    lax.fori_loop(0, STRIP // 256, block_of, 0)


def synthesize(lon_counts, lat_order, depth, diagonal, fourier, above, pair_row, basis):
    whole = pl.BlockSpec(memory_space=pltpu.VMEM)
    scalar = pl.BlockSpec(memory_space=pltpu.SMEM)
    grid_line = pl.BlockSpec((1, 8, LON_PAD), lambda i: (i, 0, 0))
    return pl.pallas_call(
        synthesis_kernel,
        grid=(2,),
        out_shape=[jax.ShapeDtypeStruct((2, 8, LON_PAD), jnp.float32)] * 5,
        in_specs=[scalar] * 4 + [whole] * 3 + [pl.BlockSpec(memory_space=pl.ANY)],
        out_specs=[grid_line] * 5,
        scratch_shapes=[
            pltpu.VMEM((2, 2, 2, WAVES, STRIP), jnp.bfloat16),
            pltpu.VMEM((2, STRIPS * 40, WAVES), jnp.bfloat16),
            pltpu.VMEM((2, STRIPS * 40, WAVES), jnp.bfloat16),
            pltpu.VMEM((2, 8, WAVES), jnp.float32),
            pltpu.VMEM((6, 8, WAVES), jnp.float32),
            pltpu.VMEM((3, 4, 640), jnp.float32),
            pltpu.SemaphoreType.DMA((2,)),
        ],
        compiler_params=pltpu.CompilerParams(vmem_limit_bytes=50 * 2**20),
    )(lon_counts, lat_order, depth, diagonal, fourier, above, pair_row, basis)


def body(
    spectral, legendre, pair_list, lon_counts, lat_order, layer_depth_log, diagonal_layer_factor
):
    rows = jnp.transpose(spectral, (0, 2, 1, 3)).reshape(6, 648, 640)
    polynomials = jnp.transpose(legendre, (0, 2, 1))
    pair_row = pair_list.reshape(1, 640)
    row = jnp.arange(64)
    slots = (
        (row[:, None] % 2 == row[None, :] // 32)
        & (jnp.repeat(lat_order, 2)[:, None] == row[None, :] % 32)
    ).astype(jnp.bfloat16)
    fourier, above, basis = exchange(
        pair_list, lon_counts, lat_order, layer_depth_log, rows, polynomials, pair_row, slots
    )
    return tuple(
        synthesize(lon_counts, lat_order, layer_depth_log, diagonal_layer_factor, fourier,
                   above.reshape(16, 4, 128), pair_row, basis)
    )


def solution(mesh):
    placed = (
        P(None, "lev", "wave", None),
        P("wave", None, None),
        P(),
        P(),
        P(),
        P("lev"),
        P("lev"),
    )
    return jax.shard_map(
        body,
        mesh=mesh,
        in_specs=placed,
        out_specs=(P("wave", "lev", None),) * 5,
        check_vma=False,
    )
```

```python
import functools

import jax
import jax.numpy as jnp
from jax import lax
from jax.experimental import pallas as pl
from jax.experimental.pallas import tpu as pltpu
from jax.sharding import PartitionSpec as P

TRUNC = 1279
ROWS = 1281
LON_PAD = 5376
WAVES = 1280
STRIP = 768
STRIPS = LON_PAD // STRIP
PEERS = 16
SHARE = 40
HALVES = (320, 328)
ORDER = ((2, 2), (1, 0), (3, 0), (0, 1), (0, 3), (1, 2), (3, 2), (2, 1), (2, 3), (2, 0), (0, 2),
         (1, 1), (3, 3), (1, 3), (3, 1))
MESH = pl.DeviceIdType.MESH

COS_TERMS = (1.0, -19.73920440673828, 64.93911743164062, -85.45011138916016,
             60.16740036010742, -25.966703414916992, 6.5273566246032715)
SIN_TERMS = (6.2831854820251465, -41.34170150756836, 81.60513305664062, -76.7030029296875,
             42.02582931518555, -14.899463653564453, 3.2375807762145996)


def turn(product, circle):
    inverse = 1.0 / circle
    part = (product - jnp.floor(product * inverse + 0.5) * circle) * inverse
    square = part * part
    cosine = jnp.full_like(square, COS_TERMS[-1])
    sine = jnp.full_like(square, SIN_TERMS[-1])
    for term in COS_TERMS[-2::-1]:
        cosine = cosine * square + term
    for term in SIN_TERMS[-2::-1]:
        sine = sine * square + term
    return cosine, sine * part


def halves(value):
    high = value.astype(jnp.bfloat16)
    return high, (value - high.astype(jnp.float32)).astype(jnp.bfloat16)


def exchange_kernel(pairs, lon_counts, lat_order, depth, spectral, legendre,
                    out_fourier, pair_row, out_basis,
                    spec, legs, send_a, send_b, got_a, got_b, stage, rights, lefts, shuffle,
                    summed, slots, send_f, got_f, send_c, got_c, column, table,
                    in_sem, leg_sem, spec_send, spec_recv, spec_own, four_send, four_recv, four_own,
                    lev_send, lev_recv, table_sem):
    wave, lev = lax.axis_index("wave"), lax.axis_index("lev")
    across, along = wave // 4, lax.rem(wave, 4)
    times = functools.partial(jnp.dot, preferred_element_type=jnp.float32)

    loads = []
    for part in (1, 0):
        load = pltpu.make_async_copy(spectral.at[pl.ds(3 * part, 3)], spec.at[pl.ds(3 * part, 3)],
                                     in_sem.at[part])
        load.start()
        loads.append(load)
    leg_load = pltpu.make_async_copy(legendre, legs, leg_sem)
    leg_load.start()

    barrier = pltpu.get_barrier_semaphore()
    for step in range(1, PEERS):
        pl.semaphore_signal(barrier, inc=1, device_id=(lax.rem(wave + step, PEERS), lev),
                            device_id_type=MESH)
        pl.semaphore_signal(barrier, inc=1, device_id=(wave, lax.rem(lev + step, PEERS)),
                            device_id_type=MESH)

    def window(duo):
        return jnp.minimum((80 * duo) // 128, 3) * 128

    def shuffle_rows(duo, _):
        lane = lax.broadcasted_iota(jnp.int32, (1, 256), 1)
        second = jnp.where(lane >= 128, 1, 0)
        inner = lane - 128 * second
        third = jnp.where(inner >= 40, 1, 0) + jnp.where(inner >= 80, 1, 0) + jnp.where(inner >= 120, 1, 0)
        source = 80 * duo - window(duo) + 40 * second + inner - 40 * third
        row = lax.broadcasted_iota(jnp.int32, (256, 256), 0)
        for place in range(3):
            wanted = jnp.where(third == place, source, -1)
            shuffle[duo, place] = jnp.where(row == wanted, 1.0, 0.0).astype(jnp.bfloat16)
        return 0

    lax.fori_loop(0, 8, shuffle_rows, 0)
    pl.semaphore_wait(barrier, 2 * (PEERS - 1))

    copies = []
    waits = {}
    for part in (1, 0):
        loads[1 - part].wait()
        for half, (rows, send, got) in enumerate(zip(HALVES, (send_a, send_b), (got_a, got_b))):
            first = half * HALVES[0]

            def shuffled(duo, _, part=part, first=first, rows=rows, send=send):
                lanes = pl.ds(pl.multiple_of(window(duo), 128), 256)
                total = times(spec[3 * part, first : first + rows, lanes], shuffle[duo, 0])
                for place in (1, 2):
                    total = total + times(spec[3 * part + place, first : first + rows, lanes],
                                          shuffle[duo, place])
                send[part, 2 * duo] = total[:, :128].astype(jnp.bfloat16)
                send[part, 2 * duo + 1] = total[:, 128:].astype(jnp.bfloat16)
                return 0

            lax.fori_loop(0, 8, shuffled, 0)
            here = []
            for number, (x, y) in enumerate(ORDER):
                other = lax.rem(across + x, 4) * 4 + lax.rem(along + y, 4)
                copy = pltpu.make_async_remote_copy(
                    src_ref=send.at[part, other], dst_ref=got.at[part, wave],
                    send_sem=spec_send.at[part, half, number], recv_sem=spec_recv.at[part, half, number],
                    device_id=(other, lev), device_id_type=MESH)
                copy.start()
                here.append(copy)
            own = pltpu.make_async_copy(send.at[part, wave], got.at[part, wave], spec_own.at[part, half])
            own.start()
            waits[part, half] = (here, own)
            copies += here

    leg_load.wait()

    def masked(place, _):
        boundary = TRUNC + 1 - pairs[wave * SHARE + place]
        values = legs[place].astype(jnp.float32)
        row = lax.broadcasted_iota(jnp.int32, values.shape, 1)
        low = jnp.where(row < boundary, values, 0.0)
        high = jnp.where((row >= boundary) & (row < ROWS), values, 0.0)
        lefts[pl.ds(pl.multiple_of(place * 64, 64), 32), :] = low.astype(jnp.bfloat16)
        lefts[pl.ds(pl.multiple_of(place * 64 + 32, 32), 32), :] = high.astype(jnp.bfloat16)
        return 0

    lax.fori_loop(0, SHARE, masked, 0)
    lane = lax.broadcasted_iota(jnp.int32, (8, 128), 1)
    for tile in range(5):
        def listed(step, values, tile=tile):
            for place in range(8):
                at = step * 8 + place
                values = jnp.where(lane == at, pairs[tile * 128 + at], values)
            return values

        values = lax.fori_loop(0, 16, listed, jnp.zeros((8, 128), jnp.int32)).astype(jnp.float32)
        pair_row[:, tile * 128 : tile * 128 + 128] = values
        column[tile * 128 : tile * 128 + 128, :] = jnp.transpose(jnp.broadcast_to(values[:1], (128, 128)))
    row = lax.broadcasted_iota(jnp.int32, (64, 64), 0)
    spot = lax.broadcasted_iota(jnp.int32, (64, 64), 1)
    wanted = jnp.zeros((64, 64), jnp.int32)
    for number in range(32):
        here = (row % 16 == number // 2) & (row // 32 == number % 2)
        wanted = jnp.where(here, lat_order[number], wanted)
    wanted = wanted + 32 * ((row // 16) % 2)
    slots[...] = jnp.where(spot == wanted, 1.0, 0.0).astype(jnp.bfloat16)
    send_f[...] = jnp.zeros_like(send_f)

    def table_copy(lat, block):
        slot = lax.rem(block, 2)
        return pltpu.make_async_copy(
            table.at[slot], out_basis.at[lat, :, :, pl.ds(pl.multiple_of(block * 128, 128), 128), :],
            table_sem.at[slot])

    def tables(lat):
        whole = lon_counts[lat_order[2 * wave + lat]]
        circle = jnp.full((1, 1), whole, jnp.int32).astype(jnp.float32)

        def block_of(block, _):
            slot = lax.rem(block, 2)

            @pl.when(block >= 2)
            def _():
                table_copy(lat, block - 2).wait()

            low = block < 5
            at = (block - jnp.where(low, 0, 5)) * 128
            base = jnp.where(low, 0.0, float(TRUNC))
            sign = jnp.where(low, 1.0, -1.0)

            def rows_of(step, _):
                rows = pl.ds(pl.multiple_of(step * 16, 16), 16)
                strip = lax.broadcasted_iota(jnp.int32, (16, STRIP), 1).astype(jnp.float32)
                source = column[pl.ds(pl.multiple_of(at + step * 16, 16), 16), :]
                number = jnp.concatenate([base + sign * source] * (STRIP // 128), axis=1)
                cosine, sine = turn(number * strip, circle)
                table[slot, 0, 0, rows, :], table[slot, 1, 0, rows, :] = halves(cosine)
                table[slot, 0, 1, rows, :], table[slot, 1, 1, rows, :] = halves(sine)
                return 0

            lax.fori_loop(0, 8, rows_of, 0)
            table_copy(lat, block).start()
            return 0

        lax.fori_loop(0, 10, block_of, 0)
        table_copy(lat, 8).wait()
        table_copy(lat, 9).wait()

    def legendre_sums(part):
        for half in (0, 1):
            here, own = waits[part, half]
            for copy in here:
                copy.wait_recv()
            own.wait()

        def widen(source, _):
            stage[pl.ds(pl.multiple_of(source * 648, 8), 320), :] = got_a[part, source].astype(jnp.float32)
            stage[pl.ds(pl.multiple_of(source * 648 + 320, 8), 328), :] = got_b[part, source].astype(jnp.float32)
            return 0

        lax.fori_loop(0, PEERS, widen, 0)

        def gather(chunk, _):
            rows = pl.ds(pl.multiple_of(chunk * 144, 16), 144)
            for level in range(8):
                taken = stage[pl.ds(chunk * 1152 + level, 144, stride=8), :]
                lanes = slice(128 * (level % 2), 128 * (level % 2) + 128)
                rights[level // 2, rows, lanes] = taken.astype(jnp.bfloat16)
            return 0

        lax.fori_loop(0, 9, gather, 0)
        lane = lax.broadcasted_iota(jnp.int32, (1, 256), 1)
        inner = jnp.where(lane >= 128, lane - 128, lane)
        inner = jnp.where(inner >= 80, inner - 80, jnp.where(inner >= 40, inner - 40, inner))

        def levels(duo, _):
            def group(chunk, total):
                result = times(lefts[pl.ds(pl.multiple_of(chunk * 512, 512), 512), :], rights[duo])
                for place in range(8):
                    total = total + jnp.where(inner == chunk * 8 + place,
                                              result[place * 64 : place * 64 + 64], 0.0)
                return total

            summed[duo] = lax.fori_loop(0, 5, group, jnp.zeros((64, 256), jnp.float32))
            return 0

        lax.fori_loop(0, 4, levels, 0)

    def in_order(rest):
        moved = jnp.zeros(rest.shape, jnp.float32)
        for _ in range(3):
            piece = rest.astype(jnp.bfloat16)
            rest = rest - piece.astype(jnp.float32)
            moved = moved + times(slots[...], piece)
        return moved

    def send_fourier(part):
        for duo in range(4):
            moved = in_order(summed[duo])
            for place in range(4):
                for odd in (0, 1):
                    send_f[part, pl.ds(8 * place + 2 * duo + odd, 16, stride=40), :] = (
                        moved[16 * place : 16 * place + 16, 128 * odd : 128 * odd + 128])
        here = []
        for number, (x, y) in enumerate(ORDER):
            other = lax.rem(across + x, 4) * 4 + lax.rem(along + y, 4)
            copy = pltpu.make_async_remote_copy(
                src_ref=send_f.at[part, pl.ds(pl.multiple_of(other * 40, 8), 40), :],
                dst_ref=got_f.at[part, pl.ds(pl.multiple_of(wave * 40, 8), 40), :],
                send_sem=four_send.at[part, number], recv_sem=four_recv.at[part, number],
                device_id=(other, lev), device_id_type=MESH)
            copy.start()
            here.append(copy)
        own = pltpu.make_async_copy(
            send_f.at[part, pl.ds(pl.multiple_of(wave * 40, 8), 40), :],
            got_f.at[part, pl.ds(pl.multiple_of(wave * 40, 8), 40), :], four_own.at[part])
        own.start()
        copies.extend(here)
        return here, own

    def arrived(here, own):
        for copy in here:
            copy.wait_recv()
        own.wait()

    tables(0)
    tables(1)
    legendre_sums(1)
    lower = jnp.zeros((64, 128), jnp.float32)
    for duo in range(4):
        lower = lower + depth[2 * duo] * summed[duo, :, :128] + depth[2 * duo + 1] * summed[duo, :, 128:]
    send_c[...] = lower
    lev_copies = []
    for step in range(1, PEERS):
        copy = pltpu.make_async_remote_copy(
            src_ref=send_c, dst_ref=got_c.at[lev],
            send_sem=lev_send.at[step - 1], recv_sem=lev_recv.at[step - 1],
            device_id=(wave, lax.rem(lev + step, PEERS)), device_id_type=MESH)
        copy.start()
        lev_copies.append(copy)
    first = send_fourier(1)
    legendre_sums(0)
    for copy in lev_copies:
        copy.wait_recv()
    above = jnp.zeros((64, 128), jnp.float32)
    got_c[lev] = send_c[...]
    for other in range(PEERS):
        above = above + jnp.where(other > lev, got_c[other], 0.0)
    above = in_order(above)
    for place in range(4):
        send_f[0, pl.ds(32 + place, 16, stride=40), :] = above[16 * place : 16 * place + 16]
    second = send_fourier(0)
    arrived(*first)
    arrived(*second)
    out_fourier[...] = got_f[...]
    for copy in copies + lev_copies:
        copy.wait_send()


def exchange(pairs, lon_counts, lat_order, depth, spectral, legendre):
    anywhere = pl.BlockSpec(memory_space=pl.ANY)
    vector = pl.BlockSpec(memory_space=pltpu.VMEM)
    scalar = pl.BlockSpec(memory_space=pltpu.SMEM)
    dma = pltpu.SemaphoreType.DMA
    return pl.pallas_call(
        exchange_kernel,
        out_shape=[
            jax.ShapeDtypeStruct((2, PEERS * 40, 128), jnp.float32),
            jax.ShapeDtypeStruct((8, 640), jnp.float32),
            jax.ShapeDtypeStruct((2, 2, 2, WAVES, STRIP), jnp.bfloat16),
        ],
        in_specs=[scalar] * 4 + [anywhere] * 2,
        out_specs=[vector, vector, anywhere],
        scratch_shapes=[
            pltpu.VMEM((6, 648, 640), jnp.bfloat16),
            pltpu.VMEM((SHARE, 32, 1296), jnp.bfloat16),
            pltpu.VMEM((2, PEERS, HALVES[0], 128), jnp.bfloat16),
            pltpu.VMEM((2, PEERS, HALVES[1], 128), jnp.bfloat16),
            pltpu.VMEM((2, PEERS, HALVES[0], 128), jnp.bfloat16),
            pltpu.VMEM((2, PEERS, HALVES[1], 128), jnp.bfloat16),
            pltpu.VMEM((PEERS * 648, 128), jnp.float32),
            pltpu.VMEM((4, 1296, 256), jnp.bfloat16),
            pltpu.VMEM((SHARE * 64, 1296), jnp.bfloat16),
            pltpu.VMEM((8, 3, 256, 256), jnp.bfloat16),
            pltpu.VMEM((4, 64, 256), jnp.float32),
            pltpu.VMEM((64, 64), jnp.bfloat16),
            pltpu.VMEM((2, PEERS * 40, 128), jnp.float32),
            pltpu.VMEM((2, PEERS * 40, 128), jnp.float32),
            pltpu.VMEM((64, 128), jnp.float32),
            pltpu.VMEM((PEERS, 64, 128), jnp.float32),
            pltpu.VMEM((640, 128), jnp.float32),
            pltpu.VMEM((2, 2, 2, 128, STRIP), jnp.bfloat16),
            dma((2,)), dma, dma((2, 2, 15)), dma((2, 2, 15)), dma((2, 2)),
            dma((2, 15)), dma((2, 15)), dma((2,)), dma((15,)), dma((15,)), dma((2,)),
        ],
        compiler_params=pltpu.CompilerParams(
            collective_id=0, has_side_effects=True, vmem_limit_bytes=56 * 2**20
        ),
    )(pairs, lon_counts, lat_order, depth, spectral, legendre)


def synthesis_kernel(lon_counts, lat_order, depth, diagonal, fourier_far, pair_far, basis,
                     out_v, out_d, out_t, out_s, out_h,
                     table, left_high, left_low, twist, coef, upper, fourier, pair_row, table_sem):
    lat = pl.program_id(0)
    wave_group = lax.axis_index("wave")

    def load(which):
        return pltpu.make_async_copy(basis.at[which], table.at[which], table_sem.at[which])

    @pl.when(lat == 0)
    def _():
        near = (pltpu.make_async_copy(pair_far, pair_row, table_sem.at[2]),
                pltpu.make_async_copy(fourier_far, fourier, table_sem.at[3]))
        for copy in near:
            copy.start()
        load(0).start()
        load(1).start()
        for copy in near:
            copy.wait()

    circle_whole = lon_counts[lat_order[2 * wave_group + lat]]
    circle = jnp.full((1, 1), circle_whole, jnp.int32).astype(jnp.float32)
    lane = lax.broadcasted_iota(jnp.int32, (1, 128), 1)

    def spread(take, keep, height):
        for place in range(3):
            tiles = [jnp.zeros((height, 128), jnp.float32)] * 5
            for source in range(PEERS):
                value = take(source)
                goal = source * SHARE
                tile, offset = goal // 128, goal % 128
                rolled = pltpu.roll(value, (offset - place * SHARE) % 128, 1)
                end = offset + SHARE
                tiles[tile] = jnp.where((lane >= offset) & (lane < end), rolled, tiles[tile])
                if end > 128:
                    tiles[tile + 1] = jnp.where(lane < end - 128, rolled, tiles[tile + 1])
            for tile in range(5):
                keep(place, tile, tiles[tile])

    for part in range(2):
        for side in range(2):
            def take(source, part=part, side=side):
                return fourier[part, pl.ds(pl.multiple_of(source * 40 + lat * 16 + side * 8, 8), 8), :]

            def keep(place, tile, value, part=part, side=side):
                at = side * 640 + tile * 128
                coef[3 * part + place, :, at : at + 128] = value

            spread(take, keep, 8)

    def take_above(source):
        return fourier[0, source * 40 + 32 : source * 40 + 36, :]

    def keep_above(place, tile, value):
        upper[place, :, tile * 128 : tile * 128 + 128] = value

    spread(take_above, keep_above, 4)

    pair = pair_row[:1, :]
    wave = jnp.concatenate([pair, TRUNC - pair], axis=1)
    weight = jnp.where(2.0 * wave < circle, jnp.where(wave == 0.0, 1.0, 2.0), 0.0)
    start = (lax.broadcasted_iota(jnp.int32, (8, WAVES), 0) * STRIP).astype(jnp.float32)
    cosine, sine = turn(start * wave, circle)
    twist[0] = cosine * weight
    twist[1] = sine * weight
    factor = wave * (1.0 / (TRUNC + 1))
    level_of = lax.broadcasted_iota(jnp.int32, (8, 1), 0)

    def rows_of(field):
        if field < 3:
            return coef[2 * field], coef[2 * field + 1]
        real, imaginary = coef[4], coef[5]
        if field == 3:
            return -factor * imaginary, factor * real
        higher = []
        for value, place in ((real, 1), (imaginary, 2)):
            total = jnp.broadcast_to(
                jnp.concatenate([upper[place, pl.ds(2 * lat, 1), :], upper[place, pl.ds(2 * lat + 1, 1), :]], axis=1),
                (8, WAVES))
            for level in range(8):
                share = jnp.where(level_of == level, diagonal[level],
                                  jnp.where(level_of < level, depth[level], 0.0))
                total = total + share * value[level : level + 1, :]
            higher.append(total)
        return higher[0], higher[1]

    for field in range(5):
        real, imaginary = rows_of(field)
        for strip in range(STRIPS):
            at = strip * 40 + field * 8
            cosine = twist[0, strip : strip + 1, :]
            sine = twist[1, strip : strip + 1, :]
            high, low = halves(real * cosine - imaginary * sine)
            left_high[0, at : at + 8, :] = high
            left_low[0, at : at + 8, :] = low
            high, low = halves(-(real * sine + imaginary * cosine))
            left_high[1, at : at + 8, :] = high
            left_low[1, at : at + 8, :] = low

    load(lat).wait()

    def block_of(block, _):
        first = pl.multiple_of(block * 256, 256)
        columns = pl.ds(first, 256)
        times = functools.partial(jnp.dot, preferred_element_type=jnp.float32)
        result = None
        for trig in (0, 1):
            high = table[lat, 0, trig, :, columns]
            term = (times(left_high[trig], high) + times(left_low[trig], high)
                    + times(left_high[trig], table[lat, 1, trig, :, columns]))
            result = term if result is None else result + term
        number = lax.broadcasted_iota(jnp.int32, (40, 256), 1) + first
        for strip in range(STRIPS):
            piece = jnp.where(number + strip * STRIP < circle_whole,
                              result[strip * 40 : strip * 40 + 40], 0.0)
            where = pl.ds(pl.multiple_of(first + strip * STRIP, 256), 256)
            for field, out in enumerate((out_v, out_d, out_t, out_s, out_h)):
                out[0, :, where] = piece[field * 8 : field * 8 + 8]
        return 0

    lax.fori_loop(0, STRIP // 256, block_of, 0)


def synthesize(lon_counts, lat_order, depth, diagonal, fourier, pair_row, basis):
    anywhere = pl.BlockSpec(memory_space=pl.ANY)
    scalar = pl.BlockSpec(memory_space=pltpu.SMEM)
    grid_line = pl.BlockSpec((1, 8, LON_PAD), lambda i: (i, 0, 0))
    return pl.pallas_call(
        synthesis_kernel,
        grid=(2,),
        out_shape=[jax.ShapeDtypeStruct((2, 8, LON_PAD), jnp.float32)] * 5,
        in_specs=[scalar] * 4 + [anywhere] * 3,
        out_specs=[grid_line] * 5,
        scratch_shapes=[
            pltpu.VMEM((2, 2, 2, WAVES, STRIP), jnp.bfloat16),
            pltpu.VMEM((2, STRIPS * 40, WAVES), jnp.bfloat16),
            pltpu.VMEM((2, STRIPS * 40, WAVES), jnp.bfloat16),
            pltpu.VMEM((2, 8, WAVES), jnp.float32),
            pltpu.VMEM((6, 8, WAVES), jnp.float32),
            pltpu.VMEM((3, 4, 640), jnp.float32),
            pltpu.VMEM((2, PEERS * 40, 128), jnp.float32),
            pltpu.VMEM((8, 640), jnp.float32),
            pltpu.SemaphoreType.DMA((4,)),
        ],
        compiler_params=pltpu.CompilerParams(vmem_limit_bytes=60 * 2**20),
    )(lon_counts, lat_order, depth, diagonal, fourier, pair_row, basis)


def body(
    spectral, legendre, pair_list, lon_counts, lat_order, layer_depth_log, diagonal_layer_factor
):
    rows = jnp.transpose(spectral, (0, 2, 1, 3)).reshape(6, 648, 640)
    polynomials = jnp.transpose(legendre, (0, 2, 1))
    fourier, pair_row, basis = exchange(
        pair_list, lon_counts, lat_order, layer_depth_log, rows, polynomials
    )
    return tuple(
        synthesize(lon_counts, lat_order, layer_depth_log, diagonal_layer_factor, fourier, pair_row, basis)
    )


def solution(mesh):
    placed = (
        P(None, "lev", "wave", None),
        P("wave", None, None),
        P(),
        P(),
        P(),
        P("lev"),
        P("lev"),
    )
    return jax.shard_map(
        body,
        mesh=mesh,
        in_specs=placed,
        out_specs=(P("wave", "lev", None),) * 5,
        check_vma=False,
    )
```

```python
import functools

import jax
import jax.numpy as jnp
from jax import lax
from jax.experimental import pallas as pl
from jax.experimental.pallas import tpu as pltpu
from jax.sharding import PartitionSpec as P

TRUNC = 1279
ROWS = 1281
LON_PAD = 5376
WAVES = 1280
STRIP = 768
STRIPS = LON_PAD // STRIP
PEERS = 16
SHARE = 40
HALVES = (320, 328)
ORDER = ((2, 2), (1, 0), (3, 0), (0, 1), (0, 3), (1, 2), (3, 2), (2, 1), (2, 3), (2, 0), (0, 2),
         (1, 1), (3, 3), (1, 3), (3, 1))
MESH = pl.DeviceIdType.MESH

COS_TERMS = (1.0, -19.73920440673828, 64.93911743164062, -85.45011138916016,
             60.16740036010742, -25.966703414916992, 6.5273566246032715)
SIN_TERMS = (6.2831854820251465, -41.34170150756836, 81.60513305664062, -76.7030029296875,
             42.02582931518555, -14.899463653564453, 3.2375807762145996)


def turn(product, circle):
    inverse = 1.0 / circle
    part = (product - jnp.floor(product * inverse + 0.5) * circle) * inverse
    square = part * part
    cosine = jnp.full_like(square, COS_TERMS[-1])
    sine = jnp.full_like(square, SIN_TERMS[-1])
    for term in COS_TERMS[-2::-1]:
        cosine = cosine * square + term
    for term in SIN_TERMS[-2::-1]:
        sine = sine * square + term
    return cosine, sine * part


def halves(value):
    high = value.astype(jnp.bfloat16)
    return high, (value - high.astype(jnp.float32)).astype(jnp.bfloat16)


def exchange_kernel(pairs, lon_counts, lat_order, depth, spectral, legendre,
                    out_fourier, pair_row, out_basis,
                    spec, legs, send_a, send_b, got_a, got_b, stage, rights, lefts, shuffle,
                    summed, halved, slots, send_f, got_f, send_c, got_c, column, table,
                    in_sem, leg_sem, spec_send, spec_recv, spec_own, four_send, four_recv, four_own,
                    lev_send, lev_recv, table_sem):
    wave, lev = lax.axis_index("wave"), lax.axis_index("lev")
    across, along = wave // 4, lax.rem(wave, 4)
    times = functools.partial(jnp.dot, preferred_element_type=jnp.float32)

    loads = []
    for part in (1, 0):
        load = pltpu.make_async_copy(spectral.at[pl.ds(3 * part, 3)], spec.at[pl.ds(3 * part, 3)],
                                     in_sem.at[part])
        load.start()
        loads.append(load)
    leg_load = pltpu.make_async_copy(legendre, legs, leg_sem)
    leg_load.start()

    barrier = pltpu.get_barrier_semaphore()
    for step in range(1, PEERS):
        pl.semaphore_signal(barrier, inc=1, device_id=(lax.rem(wave + step, PEERS), lev),
                            device_id_type=MESH)
        pl.semaphore_signal(barrier, inc=1, device_id=(wave, lax.rem(lev + step, PEERS)),
                            device_id_type=MESH)

    def window(duo):
        return jnp.minimum((80 * duo) // 128, 3) * 128

    def shuffle_rows(duo, _):
        lane = lax.broadcasted_iota(jnp.int32, (1, 256), 1)
        second = jnp.where(lane >= 128, 1, 0)
        inner = lane - 128 * second
        side = jnp.where(inner >= 60, 1, 0)
        inner = inner - 60 * side
        third = jnp.where(inner >= 20, 1, 0) + jnp.where(inner >= 40, 1, 0) + jnp.where(inner >= 60, 1, 0)
        source = 80 * duo - window(duo) + 40 * second + 20 * side + inner - 20 * third
        row = lax.broadcasted_iota(jnp.int32, (256, 256), 0)
        for place in range(3):
            wanted = jnp.where(third == place, source, -1)
            shuffle[duo, place] = jnp.where(row == wanted, 1.0, 0.0).astype(jnp.bfloat16)
        return 0

    lax.fori_loop(0, 8, shuffle_rows, 0)
    pl.semaphore_wait(barrier, 2 * (PEERS - 1))

    copies = []
    waits = {}
    for part in (1, 0):
        loads[1 - part].wait()
        for half, (rows, send, got) in enumerate(zip(HALVES, (send_a, send_b), (got_a, got_b))):
            first = half * HALVES[0]

            def shuffled(duo, _, part=part, first=first, rows=rows, send=send):
                lanes = pl.ds(pl.multiple_of(window(duo), 128), 256)
                total = times(spec[3 * part, first : first + rows, lanes], shuffle[duo, 0])
                for place in (1, 2):
                    total = total + times(spec[3 * part + place, first : first + rows, lanes],
                                          shuffle[duo, place])
                send[part, 2 * duo] = total[:, :128].astype(jnp.bfloat16)
                send[part, 2 * duo + 1] = total[:, 128:].astype(jnp.bfloat16)
                return 0

            lax.fori_loop(0, 8, shuffled, 0)
            here = []
            for number, (x, y) in enumerate(ORDER):
                other = lax.rem(across + x, 4) * 4 + lax.rem(along + y, 4)
                copy = pltpu.make_async_remote_copy(
                    src_ref=send.at[part, other], dst_ref=got.at[part, wave],
                    send_sem=spec_send.at[part, half, number], recv_sem=spec_recv.at[part, half, number],
                    device_id=(other, lev), device_id_type=MESH)
                copy.start()
                here.append(copy)
            own = pltpu.make_async_copy(send.at[part, wave], got.at[part, wave], spec_own.at[part, half])
            own.start()
            waits[part, half] = (here, own)
            copies += here

    leg_load.wait()

    def masked(place, _):
        boundary = TRUNC + 1 - pairs[wave * SHARE + place]
        values = legs[place].astype(jnp.float32)
        row = lax.broadcasted_iota(jnp.int32, values.shape, 1)
        low = jnp.where(row < boundary, values, 0.0)
        high = jnp.where((row >= boundary) & (row < ROWS), values, 0.0)
        lefts[pl.ds(pl.multiple_of(place * 64, 64), 32), :] = low.astype(jnp.bfloat16)
        lefts[pl.ds(pl.multiple_of(place * 64 + 32, 32), 32), :] = high.astype(jnp.bfloat16)
        return 0

    lax.fori_loop(0, SHARE, masked, 0)
    lane = lax.broadcasted_iota(jnp.int32, (8, 128), 1)
    for tile in range(5):
        def listed(step, values, tile=tile):
            for place in range(8):
                at = step * 8 + place
                values = jnp.where(lane == at, pairs[tile * 128 + at], values)
            return values

        values = lax.fori_loop(0, 16, listed, jnp.zeros((8, 128), jnp.int32)).astype(jnp.float32)
        pair_row[:, tile * 128 : tile * 128 + 128] = values
        column[tile * 128 : tile * 128 + 128, :] = jnp.transpose(jnp.broadcast_to(values[:1], (128, 128)))
    row = lax.broadcasted_iota(jnp.int32, (64, 64), 0)
    spot = lax.broadcasted_iota(jnp.int32, (64, 64), 1)
    wanted = jnp.zeros((64, 64), jnp.int32)
    for number in range(32):
        here = (row % 16 == number // 2) & (row // 32 == number % 2)
        wanted = jnp.where(here, lat_order[number], wanted)
    wanted = wanted + 32 * ((row // 16) % 2)
    slots[...] = jnp.where(spot == wanted, 1.0, 0.0).astype(jnp.bfloat16)
    send_f[...] = jnp.zeros_like(send_f)

    def table_copy(lat, block):
        slot = lax.rem(block, 2)
        return pltpu.make_async_copy(
            table.at[slot], out_basis.at[lat, :, :, pl.ds(pl.multiple_of(block * 128, 128), 128), :],
            table_sem.at[slot])

    def tables(lat):
        whole = lon_counts[lat_order[2 * wave + lat]]
        circle = jnp.full((1, 1), whole, jnp.int32).astype(jnp.float32)

        def block_of(block, _):
            slot = lax.rem(block, 2)

            @pl.when(block >= 2)
            def _():
                table_copy(lat, block - 2).wait()

            low = block < 5
            at = (block - jnp.where(low, 0, 5)) * 128
            base = jnp.where(low, 0.0, float(TRUNC))
            sign = jnp.where(low, 1.0, -1.0)

            def rows_of(step, _):
                rows = pl.ds(pl.multiple_of(step * 16, 16), 16)
                strip = lax.broadcasted_iota(jnp.int32, (16, STRIP), 1).astype(jnp.float32)
                source = column[pl.ds(pl.multiple_of(at + step * 16, 16), 16), :]
                number = jnp.concatenate([base + sign * source] * (STRIP // 128), axis=1)
                cosine, sine = turn(number * strip, circle)
                table[slot, 0, 0, rows, :], table[slot, 1, 0, rows, :] = halves(cosine)
                table[slot, 0, 1, rows, :], table[slot, 1, 1, rows, :] = halves(sine)
                return 0

            lax.fori_loop(0, 8, rows_of, 0)
            table_copy(lat, block).start()
            return 0

        lax.fori_loop(0, 10, block_of, 0)
        table_copy(lat, 8).wait()
        table_copy(lat, 9).wait()

    def legendre_sums(part):
        for half in (0, 1):
            here, own = waits[part, half]
            for copy in here:
                copy.wait_recv()
            own.wait()

        def widen(source, _):
            stage[pl.ds(pl.multiple_of(source * 648, 8), 320), :] = got_a[part, source].astype(jnp.float32)
            stage[pl.ds(pl.multiple_of(source * 648 + 320, 8), 328), :] = got_b[part, source].astype(jnp.float32)
            return 0

        lax.fori_loop(0, PEERS, widen, 0)

        def gather(chunk, _):
            rows = pl.ds(pl.multiple_of(chunk * 144, 16), 144)
            for duo in range(4):
                even = stage[pl.ds(chunk * 1152 + 2 * duo, 144, stride=8), :]
                odd = stage[pl.ds(chunk * 1152 + 2 * duo + 1, 144, stride=8), :]
                lower = jnp.where(left_lane, even, pltpu.roll(odd, 64, 1))
                upper = jnp.where(left_lane, pltpu.roll(even, 68, 1), pltpu.roll(odd, 4, 1))
                lanes = slice(128 * (duo % 2), 128 * (duo % 2) + 128)
                rights[duo // 2, rows, lanes] = lower.astype(jnp.bfloat16)
                rights[2 + duo // 2, rows, lanes] = upper.astype(jnp.bfloat16)
            return 0

        left_lane = lax.broadcasted_iota(jnp.int32, (1, 128), 1) < 64
        lax.fori_loop(0, 9, gather, 0)
        inner = lax.broadcasted_iota(jnp.int32, (1, 256), 1)
        for step in (128, 64, 40, 20):
            inner = jnp.where(inner >= step, inner - step, inner)

        def levels(block, _):
            side = block // 2

            def group(chunk, total):
                first = pl.multiple_of(side * 1280 + chunk * 640, 128)
                result = times(lefts[pl.ds(first, 640), :], rights[block])
                for place in range(10):
                    total = total + jnp.where(inner == chunk * 10 + place,
                                              result[place * 64 : place * 64 + 64], 0.0)
                return total

            total = lax.fori_loop(0, 2, group, jnp.zeros((64, 256), jnp.float32))
            halved[block] = total
            return 0

        lax.fori_loop(0, 4, levels, 0)
        for duo in range(4):
            lanes = slice(128 * (duo % 2), 128 * (duo % 2) + 128)
            lower, upper = halved[duo // 2, :, lanes], halved[2 + duo // 2, :, lanes]
            summed[duo, :, :128] = jnp.where(left_lane, lower, pltpu.roll(upper, 64, 1))
            summed[duo, :, 128:] = jnp.where(left_lane, pltpu.roll(lower, 64, 1), upper)

    def in_order(rest):
        moved = jnp.zeros(rest.shape, jnp.float32)
        for _ in range(3):
            piece = rest.astype(jnp.bfloat16)
            rest = rest - piece.astype(jnp.float32)
            moved = moved + times(slots[...], piece)
        return moved

    def send_fourier(part):
        for duo in range(4):
            moved = in_order(summed[duo])
            for place in range(4):
                for odd in (0, 1):
                    send_f[part, pl.ds(8 * place + 2 * duo + odd, 16, stride=40), :] = (
                        moved[16 * place : 16 * place + 16, 128 * odd : 128 * odd + 128])
        here = []
        for number, (x, y) in enumerate(ORDER):
            other = lax.rem(across + x, 4) * 4 + lax.rem(along + y, 4)
            copy = pltpu.make_async_remote_copy(
                src_ref=send_f.at[part, pl.ds(pl.multiple_of(other * 40, 8), 40), :],
                dst_ref=got_f.at[part, pl.ds(pl.multiple_of(wave * 40, 8), 40), :],
                send_sem=four_send.at[part, number], recv_sem=four_recv.at[part, number],
                device_id=(other, lev), device_id_type=MESH)
            copy.start()
            here.append(copy)
        own = pltpu.make_async_copy(
            send_f.at[part, pl.ds(pl.multiple_of(wave * 40, 8), 40), :],
            got_f.at[part, pl.ds(pl.multiple_of(wave * 40, 8), 40), :], four_own.at[part])
        own.start()
        copies.extend(here)
        return here, own

    def arrived(here, own):
        for copy in here:
            copy.wait_recv()
        own.wait()

    tables(0)
    tables(1)
    legendre_sums(1)
    lower = jnp.zeros((64, 128), jnp.float32)
    for duo in range(4):
        lower = lower + depth[2 * duo] * summed[duo, :, :128] + depth[2 * duo + 1] * summed[duo, :, 128:]
    send_c[...] = lower
    lev_copies = []
    for step in range(1, PEERS):
        copy = pltpu.make_async_remote_copy(
            src_ref=send_c, dst_ref=got_c.at[lev],
            send_sem=lev_send.at[step - 1], recv_sem=lev_recv.at[step - 1],
            device_id=(wave, lax.rem(lev + step, PEERS)), device_id_type=MESH)
        copy.start()
        lev_copies.append(copy)
    first = send_fourier(1)
    legendre_sums(0)
    for copy in lev_copies:
        copy.wait_recv()
    above = jnp.zeros((64, 128), jnp.float32)
    got_c[lev] = send_c[...]
    for other in range(PEERS):
        above = above + jnp.where(other > lev, got_c[other], 0.0)
    above = in_order(above)
    for place in range(4):
        send_f[0, pl.ds(32 + place, 16, stride=40), :] = above[16 * place : 16 * place + 16]
    second = send_fourier(0)
    arrived(*first)
    arrived(*second)
    out_fourier[...] = got_f[...]
    for copy in copies + lev_copies:
        copy.wait_send()


def exchange(pairs, lon_counts, lat_order, depth, spectral, legendre):
    anywhere = pl.BlockSpec(memory_space=pl.ANY)
    vector = pl.BlockSpec(memory_space=pltpu.VMEM)
    scalar = pl.BlockSpec(memory_space=pltpu.SMEM)
    dma = pltpu.SemaphoreType.DMA
    return pl.pallas_call(
        exchange_kernel,
        out_shape=[
            jax.ShapeDtypeStruct((2, PEERS * 40, 128), jnp.float32),
            jax.ShapeDtypeStruct((8, 640), jnp.float32),
            jax.ShapeDtypeStruct((2, 2, 2, WAVES, STRIP), jnp.bfloat16),
        ],
        in_specs=[scalar] * 4 + [anywhere] * 2,
        out_specs=[vector, vector, anywhere],
        scratch_shapes=[
            pltpu.VMEM((6, 648, 640), jnp.bfloat16),
            pltpu.VMEM((SHARE, 32, 1296), jnp.bfloat16),
            pltpu.VMEM((2, PEERS, HALVES[0], 128), jnp.bfloat16),
            pltpu.VMEM((2, PEERS, HALVES[1], 128), jnp.bfloat16),
            pltpu.VMEM((2, PEERS, HALVES[0], 128), jnp.bfloat16),
            pltpu.VMEM((2, PEERS, HALVES[1], 128), jnp.bfloat16),
            pltpu.VMEM((PEERS * 648, 128), jnp.float32),
            pltpu.VMEM((4, 1296, 256), jnp.bfloat16),
            pltpu.VMEM((SHARE * 64, 1296), jnp.bfloat16),
            pltpu.VMEM((8, 3, 256, 256), jnp.bfloat16),
            pltpu.VMEM((4, 64, 256), jnp.float32),
            pltpu.VMEM((4, 64, 256), jnp.float32),
            pltpu.VMEM((64, 64), jnp.bfloat16),
            pltpu.VMEM((2, PEERS * 40, 128), jnp.float32),
            pltpu.VMEM((2, PEERS * 40, 128), jnp.float32),
            pltpu.VMEM((64, 128), jnp.float32),
            pltpu.VMEM((PEERS, 64, 128), jnp.float32),
            pltpu.VMEM((640, 128), jnp.float32),
            pltpu.VMEM((2, 2, 2, 128, STRIP), jnp.bfloat16),
            dma((2,)), dma, dma((2, 2, 15)), dma((2, 2, 15)), dma((2, 2)),
            dma((2, 15)), dma((2, 15)), dma((2,)), dma((15,)), dma((15,)), dma((2,)),
        ],
        compiler_params=pltpu.CompilerParams(
            collective_id=0, has_side_effects=True, vmem_limit_bytes=56 * 2**20
        ),
    )(pairs, lon_counts, lat_order, depth, spectral, legendre)


def synthesis_kernel(lon_counts, lat_order, depth, diagonal, fourier_far, pair_far, basis,
                     out_v, out_d, out_t, out_s, out_h,
                     table, left, twist, coef, upper, fourier, pair_row, table_sem):
    lat = pl.program_id(0)
    wave_group = lax.axis_index("wave")

    def load(which):
        return pltpu.make_async_copy(basis.at[which], table.at[which], table_sem.at[which])

    @pl.when(lat == 0)
    def _():
        near = (pltpu.make_async_copy(pair_far, pair_row, table_sem.at[2]),
                pltpu.make_async_copy(fourier_far, fourier, table_sem.at[3]))
        for copy in near:
            copy.start()
        load(0).start()
        load(1).start()
        for copy in near:
            copy.wait()

    circle_whole = lon_counts[lat_order[2 * wave_group + lat]]
    low_rows = STRIPS * 40
    lane = lax.broadcasted_iota(jnp.int32, (1, 128), 1)

    def spread(take, keep, height):
        for place in range(3):
            tiles = [jnp.zeros((height, 128), jnp.float32)] * 5
            for source in range(PEERS):
                value = take(source)
                for side in range(2):
                    goal = source * SHARE + 20 * side
                    tile, offset = goal // 128, goal % 128
                    rolled = pltpu.roll(value, (offset - place * 20 - 64 * side) % 128, 1)
                    end = offset + 20
                    tiles[tile] = jnp.where((lane >= offset) & (lane < end), rolled, tiles[tile])
                    if end > 128:
                        tiles[tile + 1] = jnp.where(lane < end - 128, rolled, tiles[tile + 1])
            for tile in range(5):
                keep(place, tile, tiles[tile])

    def turned(which, _):
        count = lon_counts[lat_order[2 * wave_group + which]]
        circle = jnp.full((1, 1), count, jnp.int32).astype(jnp.float32)
        for part in range(2):
            for side in range(2):
                def take(source, part=part, side=side):
                    return fourier[part, pl.ds(pl.multiple_of(source * 40 + which * 16 + side * 8, 8), 8), :]

                def keep(place, tile, value, part=part, side=side):
                    at = side * 640 + tile * 128
                    coef[3 * part + place, :, at : at + 128] = value

                spread(take, keep, 8)

        def take_above(source):
            return fourier[0, source * 40 + 32 : source * 40 + 36, :]

        def keep_above(place, tile, value):
            upper[place, :, tile * 128 : tile * 128 + 128] = value

        spread(take_above, keep_above, 4)

        pair = pair_row[:1, :]
        wave = jnp.concatenate([pair, TRUNC - pair], axis=1)
        weight = jnp.where(2.0 * wave < circle, jnp.where(wave == 0.0, 1.0, 2.0), 0.0)
        start = (lax.broadcasted_iota(jnp.int32, (8, WAVES), 0) * STRIP).astype(jnp.float32)
        cosine, sine = turn(start * wave, circle)
        twist[0] = cosine * weight
        twist[1] = sine * weight
        factor = wave * (1.0 / (TRUNC + 1))
        level_of = lax.broadcasted_iota(jnp.int32, (8, 1), 0)

        def rows_of(field):
            if field < 3:
                return coef[2 * field], coef[2 * field + 1]
            real, imaginary = coef[4], coef[5]
            if field == 3:
                return -factor * imaginary, factor * real
            higher = []
            for value, place in ((real, 1), (imaginary, 2)):
                total = jnp.broadcast_to(
                    jnp.concatenate([upper[place, pl.ds(2 * which, 1), :], upper[place, pl.ds(2 * which + 1, 1), :]], axis=1),
                    (8, WAVES))
                for level in range(8):
                    share = jnp.where(level_of == level, diagonal[level],
                                      jnp.where(level_of < level, depth[level], 0.0))
                    total = total + share * value[level : level + 1, :]
                higher.append(total)
            return higher[0], higher[1]

        for field in range(5):
            real, imaginary = rows_of(field)
            for strip in range(STRIPS):
                at = strip * 40 + field * 8
                cosine = twist[0, strip : strip + 1, :]
                sine = twist[1, strip : strip + 1, :]
                high, low = halves(real * cosine - imaginary * sine)
                left[which, 0, at : at + 8, :] = high
                left[which, 0, low_rows + at : low_rows + at + 8, :] = low
                high, low = halves(-(real * sine + imaginary * cosine))
                left[which, 1, at : at + 8, :] = high
                left[which, 1, low_rows + at : low_rows + at + 8, :] = low

        return 0

    @pl.when(lat == 0)
    def _():
        lax.fori_loop(0, 2, turned, 0)

    load(lat).wait()

    def block_of(block, _):
        first = pl.multiple_of(block * 256, 256)
        columns = pl.ds(first, 256)
        times = functools.partial(jnp.dot, preferred_element_type=jnp.float32)
        result = None
        for trig in (0, 1):
            high = table[lat, 0, trig, :, columns]
            both = times(left[lat, trig], high)
            term = (both[:low_rows] + both[low_rows:]
                    + times(left[lat, trig, :low_rows], table[lat, 1, trig, :, columns]))
            result = term if result is None else result + term
        number = lax.broadcasted_iota(jnp.int32, (40, 256), 1) + first
        for strip in range(STRIPS):
            piece = jnp.where(number + strip * STRIP < circle_whole,
                              result[strip * 40 : strip * 40 + 40], 0.0)
            where = pl.ds(pl.multiple_of(first + strip * STRIP, 256), 256)
            for field, out in enumerate((out_v, out_d, out_t, out_s, out_h)):
                out[0, :, where] = piece[field * 8 : field * 8 + 8]
        return 0

    lax.fori_loop(0, STRIP // 256, block_of, 0)


def synthesize(lon_counts, lat_order, depth, diagonal, fourier, pair_row, basis):
    anywhere = pl.BlockSpec(memory_space=pl.ANY)
    scalar = pl.BlockSpec(memory_space=pltpu.SMEM)
    grid_line = pl.BlockSpec((1, 8, LON_PAD), lambda i: (i, 0, 0))
    return pl.pallas_call(
        synthesis_kernel,
        grid=(2,),
        out_shape=[jax.ShapeDtypeStruct((2, 8, LON_PAD), jnp.float32)] * 5,
        in_specs=[scalar] * 4 + [anywhere] * 3,
        out_specs=[grid_line] * 5,
        scratch_shapes=[
            pltpu.VMEM((2, 2, 2, WAVES, STRIP), jnp.bfloat16),
            pltpu.VMEM((2, 2, STRIPS * 80, WAVES), jnp.bfloat16),
            pltpu.VMEM((2, 8, WAVES), jnp.float32),
            pltpu.VMEM((6, 8, WAVES), jnp.float32),
            pltpu.VMEM((3, 4, 640), jnp.float32),
            pltpu.VMEM((2, PEERS * 40, 128), jnp.float32),
            pltpu.VMEM((8, 640), jnp.float32),
            pltpu.SemaphoreType.DMA((4,)),
        ],
        compiler_params=pltpu.CompilerParams(vmem_limit_bytes=60 * 2**20),
    )(lon_counts, lat_order, depth, diagonal, fourier, pair_row, basis)


def body(
    spectral, legendre, pair_list, lon_counts, lat_order, layer_depth_log, diagonal_layer_factor
):
    rows = jnp.transpose(spectral, (0, 2, 1, 3)).reshape(6, 648, 640)
    polynomials = jnp.transpose(legendre, (0, 2, 1))
    fourier, pair_row, basis = exchange(
        pair_list, lon_counts, lat_order, layer_depth_log, rows, polynomials
    )
    return tuple(
        synthesize(lon_counts, lat_order, layer_depth_log, diagonal_layer_factor, fourier, pair_row, basis)
    )


def solution(mesh):
    placed = (
        P(None, "lev", "wave", None),
        P("wave", None, None),
        P(),
        P(),
        P(),
        P("lev"),
        P("lev"),
    )
    return jax.shard_map(
        body,
        mesh=mesh,
        in_specs=placed,
        out_specs=(P("wave", "lev", None),) * 5,
        check_vma=False,
    )
```

```python
import functools

import jax
import jax.numpy as jnp
from jax import lax
from jax.experimental import pallas as pl
from jax.experimental.pallas import tpu as pltpu
from jax.sharding import PartitionSpec as P

TRUNC = 1279
ROWS = 1281
LON_PAD = 5376
WAVES = 1280
STRIP = 768
STRIPS = LON_PAD // STRIP
PEERS = 16
SHARE = 40
HALVES = (320, 328)
ORDER = ((2, 2), (1, 0), (3, 0), (0, 1), (0, 3), (1, 2), (3, 2), (2, 1), (2, 3), (2, 0), (0, 2),
         (1, 1), (3, 3), (1, 3), (3, 1))
MESH = pl.DeviceIdType.MESH

COS_TERMS = (1.0, -19.73920440673828, 64.93911743164062, -85.45011138916016,
             60.16740036010742, -25.966703414916992, 6.5273566246032715)
SIN_TERMS = (6.2831854820251465, -41.34170150756836, 81.60513305664062, -76.7030029296875,
             42.02582931518555, -14.899463653564453, 3.2375807762145996)


def turn(product, circle):
    inverse = 1.0 / circle
    part = (product - jnp.floor(product * inverse + 0.5) * circle) * inverse
    square = part * part
    cosine = jnp.full_like(square, COS_TERMS[-1])
    sine = jnp.full_like(square, SIN_TERMS[-1])
    for term in COS_TERMS[-2::-1]:
        cosine = cosine * square + term
    for term in SIN_TERMS[-2::-1]:
        sine = sine * square + term
    return cosine, sine * part


def halves(value):
    high = value.astype(jnp.bfloat16)
    return high, (value - high.astype(jnp.float32)).astype(jnp.bfloat16)


def exchange_kernel(pairs, lon_counts, lat_order, depth, spectral, legendre,
                    out_fourier, pair_row, warm_t, warm_s, out_basis,
                    spec, legs, send_a, send_b, got_a, got_b, stage, rights, lefts, shuffle,
                    summed, halved, slots, send_f, got_f, send_c, got_c, column, table, coef, twist, left,
                    in_sem, leg_sem, spec_send, spec_recv, spec_own, four_send, four_recv, four_own,
                    lev_send, lev_recv, table_sem):
    wave, lev = lax.axis_index("wave"), lax.axis_index("lev")
    across, along = wave // 4, lax.rem(wave, 4)
    times = functools.partial(jnp.dot, preferred_element_type=jnp.float32)

    loads = []
    for part in (1, 0):
        load = pltpu.make_async_copy(spectral.at[pl.ds(3 * part, 3)], spec.at[pl.ds(3 * part, 3)],
                                     in_sem.at[part])
        load.start()
        loads.append(load)
    leg_load = pltpu.make_async_copy(legendre, legs, leg_sem)
    leg_load.start()

    barrier = pltpu.get_barrier_semaphore()
    for step in range(1, PEERS):
        pl.semaphore_signal(barrier, inc=1, device_id=(lax.rem(wave + step, PEERS), lev),
                            device_id_type=MESH)
        pl.semaphore_signal(barrier, inc=1, device_id=(wave, lax.rem(lev + step, PEERS)),
                            device_id_type=MESH)

    def window(duo):
        return jnp.minimum((80 * duo) // 128, 3) * 128

    def shuffle_rows(owner):
        duo, second = owner // 2, lax.rem(owner, 2)
        lane = lax.broadcasted_iota(jnp.int32, (1, 128), 1)
        side = jnp.where(lane >= 60, 1, 0)
        inner = lane - 60 * side
        third = jnp.where(inner >= 20, 1, 0) + jnp.where(inner >= 40, 1, 0) + jnp.where(inner >= 60, 1, 0)
        source = 80 * duo - window(duo) + 40 * second + 20 * side + inner - 20 * third
        row = lax.broadcasted_iota(jnp.int32, (256, 128), 0)
        lanes = pl.ds(pl.multiple_of(second * 128, 128), 128)
        for place in range(3):
            wanted = jnp.where(third == place, source, -1)
            shuffle[duo, place, :, lanes] = jnp.where(row == wanted, 1.0, 0.0).astype(jnp.bfloat16)

    def shuffled_first(owner):
        duo = owner // 2
        lanes = pl.ds(pl.multiple_of(lax.rem(owner, 2) * 128, 128), 128)
        source = pl.ds(pl.multiple_of(window(duo), 128), 256)
        total = None
        for place in range(3):
            term = times(spec[3 + place, : HALVES[0], source], shuffle[duo, place, :, lanes])
            total = term if total is None else total + term
        send_a[1, owner] = total.astype(jnp.bfloat16)

    def owner_of(x, y):
        return lax.rem(across + x, 4) * 4 + lax.rem(along + y, 4)


    copies = []
    waits = {}
    for part in (1, 0):
        loads[1 - part].wait()
        for half, (rows, send, got) in enumerate(zip(HALVES, (send_a, send_b), (got_a, got_b))):
            first = half * HALVES[0]

            def shuffled(duo, _, part=part, first=first, rows=rows, send=send):
                lanes = pl.ds(pl.multiple_of(window(duo), 128), 256)
                total = times(spec[3 * part, first : first + rows, lanes], shuffle[duo, 0])
                for place in (1, 2):
                    total = total + times(spec[3 * part + place, first : first + rows, lanes],
                                          shuffle[duo, place])
                send[part, 2 * duo] = total[:, :128].astype(jnp.bfloat16)
                send[part, 2 * duo + 1] = total[:, 128:].astype(jnp.bfloat16)
                return 0

            opening = part == 1 and half == 0
            if not opening:
                lax.fori_loop(0, 8, shuffled, 0)
            here = []
            for number, (x, y) in enumerate(ORDER):
                other = owner_of(x, y)
                if opening:
                    shuffle_rows(other)
                    shuffled_first(other)
                    if number == 0:
                        pl.semaphore_wait(barrier, 2 * (PEERS - 1))
                copy = pltpu.make_async_remote_copy(
                    src_ref=send.at[part, other], dst_ref=got.at[part, wave],
                    send_sem=spec_send.at[part, half, number], recv_sem=spec_recv.at[part, half, number],
                    device_id=(other, lev), device_id_type=MESH)
                copy.start()
                here.append(copy)
            if opening:
                shuffle_rows(wave)
                shuffled_first(wave)
            own = pltpu.make_async_copy(send.at[part, wave], got.at[part, wave], spec_own.at[part, half])
            own.start()
            waits[part, half] = (here, own)
            copies += here

    leg_load.wait()

    def masked(place, _):
        boundary = TRUNC + 1 - pairs[wave * SHARE + place]
        values = legs[place].astype(jnp.float32)
        row = lax.broadcasted_iota(jnp.int32, values.shape, 1)
        low = jnp.where(row < boundary, values, 0.0)
        high = jnp.where((row >= boundary) & (row < ROWS), values, 0.0)
        lefts[pl.ds(pl.multiple_of(place * 64, 64), 32), :] = low.astype(jnp.bfloat16)
        lefts[pl.ds(pl.multiple_of(place * 64 + 32, 32), 32), :] = high.astype(jnp.bfloat16)
        return 0

    lax.fori_loop(0, SHARE, masked, 0)
    lane = lax.broadcasted_iota(jnp.int32, (8, 128), 1)
    for tile in range(5):
        def listed(step, values, tile=tile):
            for place in range(8):
                at = step * 8 + place
                values = jnp.where(lane == at, pairs[tile * 128 + at], values)
            return values

        values = lax.fori_loop(0, 16, listed, jnp.zeros((8, 128), jnp.int32)).astype(jnp.float32)
        pair_row[:, tile * 128 : tile * 128 + 128] = values
        column[tile * 128 : tile * 128 + 128, :] = jnp.transpose(jnp.broadcast_to(values[:1], (128, 128)))
    row = lax.broadcasted_iota(jnp.int32, (64, 64), 0)
    spot = lax.broadcasted_iota(jnp.int32, (64, 64), 1)
    wanted = jnp.zeros((64, 64), jnp.int32)
    for number in range(32):
        here = (row % 16 == number // 2) & (row // 32 == number % 2)
        wanted = jnp.where(here, lat_order[number], wanted)
    wanted = wanted + 32 * ((row // 16) % 2)
    slots[...] = jnp.where(spot == wanted, 1.0, 0.0).astype(jnp.bfloat16)
    send_f[...] = jnp.zeros_like(send_f)

    def circle_of(lat):
        whole = lon_counts[lat_order[2 * wave + lat]]
        return whole, jnp.full((1, 1), whole, jnp.int32).astype(jnp.float32)

    def table_copy(lat):
        return pltpu.make_async_copy(table.at[lat], out_basis.at[lat], table_sem.at[lat])

    def tables(lat):
        _, circle = circle_of(lat)

        def rows_of(step, _):
            rows = pl.ds(pl.multiple_of(step * 16, 16), 16)
            mirrored = pl.ds(pl.multiple_of(step * 16 + 640, 16), 16)
            strip = lax.broadcasted_iota(jnp.int32, (16, STRIP), 1).astype(jnp.float32)
            number = jnp.concatenate([column[rows, :]] * (STRIP // 128), axis=1)
            for where, value in ((rows, number), (mirrored, TRUNC - number)):
                cosine, sine = turn(value * strip, circle)
                table[lat, 0, 0, where, :], table[lat, 1, 0, where, :] = halves(cosine)
                table[lat, 0, 1, where, :], table[lat, 1, 1, where, :] = halves(sine)
            return 0

        lax.fori_loop(0, 40, rows_of, 0)
        table_copy(lat).start()

    def twists(lat):
        _, circle = circle_of(lat)
        pair = pair_row[:1, :]
        number = jnp.concatenate([pair, TRUNC - pair], axis=1)
        weight = jnp.where(2.0 * number < circle, jnp.where(number == 0.0, 1.0, 2.0), 0.0)
        start = (lax.broadcasted_iota(jnp.int32, (8, WAVES), 0) * STRIP).astype(jnp.float32)
        cosine, sine = turn(start * number, circle)
        twist[lat, 0] = cosine * weight
        twist[lat, 1] = sine * weight

    def legendre_sums(part):
        for half in (0, 1):
            here, own = waits[part, half]
            for copy in here:
                copy.wait_recv()
            own.wait()

        def widen(source, _):
            stage[pl.ds(pl.multiple_of(source * 648, 8), 320), :] = got_a[part, source].astype(jnp.float32)
            stage[pl.ds(pl.multiple_of(source * 648 + 320, 8), 328), :] = got_b[part, source].astype(jnp.float32)
            return 0

        lax.fori_loop(0, PEERS, widen, 0)

        def gather(chunk, _):
            rows = pl.ds(pl.multiple_of(chunk * 144, 16), 144)
            for duo in range(4):
                even = stage[pl.ds(chunk * 1152 + 2 * duo, 144, stride=8), :]
                odd = stage[pl.ds(chunk * 1152 + 2 * duo + 1, 144, stride=8), :]
                lower = jnp.where(left_lane, even, pltpu.roll(odd, 64, 1))
                upper = jnp.where(left_lane, pltpu.roll(even, 68, 1), pltpu.roll(odd, 4, 1))
                lanes = slice(128 * (duo % 2), 128 * (duo % 2) + 128)
                rights[duo // 2, rows, lanes] = lower.astype(jnp.bfloat16)
                rights[2 + duo // 2, rows, lanes] = upper.astype(jnp.bfloat16)
            return 0

        left_lane = lax.broadcasted_iota(jnp.int32, (1, 128), 1) < 64
        lax.fori_loop(0, 9, gather, 0)
        inner = lax.broadcasted_iota(jnp.int32, (1, 256), 1)
        for step in (128, 64, 40, 20):
            inner = jnp.where(inner >= step, inner - step, inner)

        def levels(block, _):
            side = block // 2

            def group(chunk, total):
                first = pl.multiple_of(side * 1280 + chunk * 640, 128)
                result = times(lefts[pl.ds(first, 640), :], rights[block])
                for place in range(10):
                    total = total + jnp.where(inner == chunk * 10 + place,
                                              result[place * 64 : place * 64 + 64], 0.0)
                return total

            total = lax.fori_loop(0, 2, group, jnp.zeros((64, 256), jnp.float32))
            halved[block] = total
            return 0

        lax.fori_loop(0, 4, levels, 0)
        for duo in range(4):
            lanes = slice(128 * (duo % 2), 128 * (duo % 2) + 128)
            lower, upper = halved[duo // 2, :, lanes], halved[2 + duo // 2, :, lanes]
            summed[duo, :, :128] = jnp.where(left_lane, lower, pltpu.roll(upper, 64, 1))
            summed[duo, :, 128:] = jnp.where(left_lane, pltpu.roll(lower, 64, 1), upper)

    def in_order(rest):
        moved = jnp.zeros(rest.shape, jnp.float32)
        for _ in range(3):
            piece = rest.astype(jnp.bfloat16)
            rest = rest - piece.astype(jnp.float32)
            moved = moved + times(slots[...], piece)
        return moved

    def send_fourier(part):
        for duo in range(4):
            moved = in_order(summed[duo])
            for place in range(4):
                for odd in (0, 1):
                    send_f[part, pl.ds(8 * place + 2 * duo + odd, 16, stride=40), :] = (
                        moved[16 * place : 16 * place + 16, 128 * odd : 128 * odd + 128])
        here = []
        for number, (x, y) in enumerate(ORDER):
            other = lax.rem(across + x, 4) * 4 + lax.rem(along + y, 4)
            copy = pltpu.make_async_remote_copy(
                src_ref=send_f.at[part, pl.ds(pl.multiple_of(other * 40, 8), 40), :],
                dst_ref=got_f.at[part, pl.ds(pl.multiple_of(wave * 40, 8), 40), :],
                send_sem=four_send.at[part, number], recv_sem=four_recv.at[part, number],
                device_id=(other, lev), device_id_type=MESH)
            copy.start()
            here.append(copy)
        own = pltpu.make_async_copy(
            send_f.at[part, pl.ds(pl.multiple_of(wave * 40, 8), 40), :],
            got_f.at[part, pl.ds(pl.multiple_of(wave * 40, 8), 40), :], four_own.at[part])
        own.start()
        copies.extend(here)
        return here, own

    def arrived(here, own):
        for copy in here:
            copy.wait_recv()
        own.wait()

    line = lax.broadcasted_iota(jnp.int32, (1, 128), 1)

    def spread(take, keep, height):
        for place in range(3):
            tiles = [jnp.zeros((height, 128), jnp.float32)] * 5
            for source in range(PEERS):
                value = take(source)
                for side in range(2):
                    goal = source * SHARE + 20 * side
                    tile, offset = goal // 128, goal % 128
                    rolled = pltpu.roll(value, (offset - place * 20 - 64 * side) % 128, 1)
                    end = offset + 20
                    tiles[tile] = jnp.where((line >= offset) & (line < end), rolled, tiles[tile])
                    if end > 128:
                        tiles[tile + 1] = jnp.where(line < end - 128, rolled, tiles[tile + 1])
            for tile in range(5):
                keep(place, tile, tiles[tile])

    def warm(lat, _):
        for side in range(2):
            def take(source, side=side):
                return got_f[1, pl.ds(pl.multiple_of(source * 40 + lat * 16 + side * 8, 8), 8), :]

            def keep(place, tile, value, side=side):
                at = side * 640 + tile * 128
                coef[place, :, at : at + 128] = value

            spread(take, keep, 8)
        pair = pair_row[:1, :]
        factor = jnp.concatenate([pair, TRUNC - pair], axis=1) * (1.0 / (TRUNC + 1))
        low_rows = STRIPS * 16
        for order in range(2):
            real, imaginary = coef[1], coef[2]
            if order == 1:
                real, imaginary = -factor * imaginary, factor * real
            for strip in range(STRIPS):
                at = strip * 16 + order * 8
                cosine = twist[lat, 0, strip : strip + 1, :]
                sine = twist[lat, 1, strip : strip + 1, :]
                high, low = halves(real * cosine - imaginary * sine)
                left[0, at : at + 8, :] = high
                left[0, low_rows + at : low_rows + at + 8, :] = low
                high, low = halves(-(real * sine + imaginary * cosine))
                left[1, at : at + 8, :] = high
                left[1, low_rows + at : low_rows + at + 8, :] = low
        whole, _ = circle_of(lat)

        def block_of(block, _):
            first = pl.multiple_of(block * 256, 256)
            columns = pl.ds(first, 256)
            result = None
            for trig in (0, 1):
                both = times(left[trig], table[lat, 0, trig, :, columns])
                term = (both[:low_rows] + both[low_rows:]
                        + times(left[trig, :low_rows], table[lat, 1, trig, :, columns]))
                result = term if result is None else result + term
            number = lax.broadcasted_iota(jnp.int32, (16, 256), 1) + first
            for strip in range(STRIPS):
                piece = jnp.where(number + strip * STRIP < whole, result[strip * 16 : strip * 16 + 16], 0.0)
                where = pl.ds(pl.multiple_of(first + strip * STRIP, 256), 256)
                warm_t[lat, :, where] = piece[:8]
                warm_s[lat, :, where] = piece[8:]
            return 0

        lax.fori_loop(0, STRIP // 256, block_of, 0)
        return 0

    for lat in range(2):
        twists(lat)
        tables(lat)
    legendre_sums(1)
    lower = jnp.zeros((64, 128), jnp.float32)
    for duo in range(4):
        lower = lower + depth[2 * duo] * summed[duo, :, :128] + depth[2 * duo + 1] * summed[duo, :, 128:]
    send_c[...] = lower
    lev_copies = []
    for step in range(1, PEERS):
        copy = pltpu.make_async_remote_copy(
            src_ref=send_c, dst_ref=got_c.at[lev],
            send_sem=lev_send.at[step - 1], recv_sem=lev_recv.at[step - 1],
            device_id=(wave, lax.rem(lev + step, PEERS)), device_id_type=MESH)
        copy.start()
        lev_copies.append(copy)
    first = send_fourier(1)
    legendre_sums(0)
    for copy in lev_copies:
        copy.wait_recv()
    above = jnp.zeros((64, 128), jnp.float32)
    got_c[lev] = send_c[...]
    for other in range(PEERS):
        above = above + jnp.where(other > lev, got_c[other], 0.0)
    above = in_order(above)
    for place in range(4):
        send_f[0, pl.ds(32 + place, 16, stride=40), :] = above[16 * place : 16 * place + 16]
    second = send_fourier(0)
    arrived(*first)
    lax.fori_loop(0, 2, warm, 0)
    arrived(*second)
    out_fourier[...] = got_f[...]
    for copy in copies + lev_copies:
        copy.wait_send()
    table_copy(0).wait()
    table_copy(1).wait()


def exchange(pairs, lon_counts, lat_order, depth, spectral, legendre):
    anywhere = pl.BlockSpec(memory_space=pl.ANY)
    vector = pl.BlockSpec(memory_space=pltpu.VMEM)
    scalar = pl.BlockSpec(memory_space=pltpu.SMEM)
    dma = pltpu.SemaphoreType.DMA
    return pl.pallas_call(
        exchange_kernel,
        out_shape=[
            jax.ShapeDtypeStruct((2, PEERS * 40, 128), jnp.float32),
            jax.ShapeDtypeStruct((8, 640), jnp.float32),
            jax.ShapeDtypeStruct((2, 8, LON_PAD), jnp.float32),
            jax.ShapeDtypeStruct((2, 8, LON_PAD), jnp.float32),
            jax.ShapeDtypeStruct((2, 2, 2, WAVES, STRIP), jnp.bfloat16),
        ],
        in_specs=[scalar] * 4 + [anywhere] * 2,
        out_specs=[vector] * 4 + [anywhere],
        scratch_shapes=[
            pltpu.VMEM((6, 648, 640), jnp.bfloat16),
            pltpu.VMEM((SHARE, 32, 1296), jnp.bfloat16),
            pltpu.VMEM((2, PEERS, HALVES[0], 128), jnp.bfloat16),
            pltpu.VMEM((2, PEERS, HALVES[1], 128), jnp.bfloat16),
            pltpu.VMEM((2, PEERS, HALVES[0], 128), jnp.bfloat16),
            pltpu.VMEM((2, PEERS, HALVES[1], 128), jnp.bfloat16),
            pltpu.VMEM((PEERS * 648, 128), jnp.float32),
            pltpu.VMEM((4, 1296, 256), jnp.bfloat16),
            pltpu.VMEM((SHARE * 64, 1296), jnp.bfloat16),
            pltpu.VMEM((8, 3, 256, 256), jnp.bfloat16),
            pltpu.VMEM((4, 64, 256), jnp.float32),
            pltpu.VMEM((4, 64, 256), jnp.float32),
            pltpu.VMEM((64, 64), jnp.bfloat16),
            pltpu.VMEM((2, PEERS * 40, 128), jnp.float32),
            pltpu.VMEM((2, PEERS * 40, 128), jnp.float32),
            pltpu.VMEM((64, 128), jnp.float32),
            pltpu.VMEM((PEERS, 64, 128), jnp.float32),
            pltpu.VMEM((640, 128), jnp.float32),
            pltpu.VMEM((2, 2, 2, WAVES, STRIP), jnp.bfloat16),
            pltpu.VMEM((3, 8, WAVES), jnp.float32),
            pltpu.VMEM((2, 2, 8, WAVES), jnp.float32),
            pltpu.VMEM((2, STRIPS * 32, WAVES), jnp.bfloat16),
            dma((2,)), dma, dma((2, 2, 15)), dma((2, 2, 15)), dma((2, 2)),
            dma((2, 15)), dma((2, 15)), dma((2,)), dma((15,)), dma((15,)), dma((2,)),
        ],
        compiler_params=pltpu.CompilerParams(
            collective_id=0, has_side_effects=True, vmem_limit_bytes=60 * 2**20
        ),
    )(pairs, lon_counts, lat_order, depth, spectral, legendre)


def synthesis_kernel(lon_counts, lat_order, depth, diagonal, fourier_far, pair_far, warm_t, warm_s, basis,
                     out_v, out_d, out_t, out_s, out_h,
                     table, left, twist, coef, upper, fourier, pair_row, table_sem):
    lat = pl.program_id(0)
    wave_group = lax.axis_index("wave")

    def load(which):
        return pltpu.make_async_copy(basis.at[which], table.at[which], table_sem.at[which])

    passed = (pltpu.make_async_copy(warm_t, out_t, table_sem.at[4]),
              pltpu.make_async_copy(warm_s, out_s, table_sem.at[5]))

    @pl.when(lat == 0)
    def _():
        near = (pltpu.make_async_copy(pair_far, pair_row, table_sem.at[2]),
                pltpu.make_async_copy(fourier_far, fourier, table_sem.at[3]))
        for copy in near:
            copy.start()
        load(0).start()
        load(1).start()
        for copy in passed:
            copy.start()
        for copy in near:
            copy.wait()

    circle_whole = lon_counts[lat_order[2 * wave_group + lat]]
    low_rows = STRIPS * 24
    lane = lax.broadcasted_iota(jnp.int32, (1, 128), 1)

    def spread(take, keep, height):
        for place in range(3):
            tiles = [jnp.zeros((height, 128), jnp.float32)] * 5
            for source in range(PEERS):
                value = take(source)
                for side in range(2):
                    goal = source * SHARE + 20 * side
                    tile, offset = goal // 128, goal % 128
                    rolled = pltpu.roll(value, (offset - place * 20 - 64 * side) % 128, 1)
                    end = offset + 20
                    tiles[tile] = jnp.where((lane >= offset) & (lane < end), rolled, tiles[tile])
                    if end > 128:
                        tiles[tile + 1] = jnp.where(lane < end - 128, rolled, tiles[tile + 1])
            for tile in range(5):
                keep(place, tile, tiles[tile])

    def turned(which, _):
        count = lon_counts[lat_order[2 * wave_group + which]]
        circle = jnp.full((1, 1), count, jnp.int32).astype(jnp.float32)
        for part in range(2):
            for side in range(2):
                def take(source, part=part, side=side):
                    return fourier[part, pl.ds(pl.multiple_of(source * 40 + which * 16 + side * 8, 8), 8), :]

                def keep(place, tile, value, part=part, side=side):
                    at = side * 640 + tile * 128
                    coef[3 * part + place, :, at : at + 128] = value

                spread(take, keep, 8)

        def take_above(source):
            return fourier[0, source * 40 + 32 : source * 40 + 36, :]

        def keep_above(place, tile, value):
            upper[place, :, tile * 128 : tile * 128 + 128] = value

        spread(take_above, keep_above, 4)

        pair = pair_row[:1, :]
        wave = jnp.concatenate([pair, TRUNC - pair], axis=1)
        weight = jnp.where(2.0 * wave < circle, jnp.where(wave == 0.0, 1.0, 2.0), 0.0)
        start = (lax.broadcasted_iota(jnp.int32, (8, WAVES), 0) * STRIP).astype(jnp.float32)
        cosine, sine = turn(start * wave, circle)
        twist[0] = cosine * weight
        twist[1] = sine * weight
        level_of = lax.broadcasted_iota(jnp.int32, (8, 1), 0)

        def rows_of(field):
            if field < 2:
                return coef[2 * field], coef[2 * field + 1]
            real, imaginary = coef[4], coef[5]
            higher = []
            for value, place in ((real, 1), (imaginary, 2)):
                total = jnp.broadcast_to(
                    jnp.concatenate([upper[place, pl.ds(2 * which, 1), :], upper[place, pl.ds(2 * which + 1, 1), :]], axis=1),
                    (8, WAVES))
                for level in range(8):
                    share = jnp.where(level_of == level, diagonal[level],
                                      jnp.where(level_of < level, depth[level], 0.0))
                    total = total + share * value[level : level + 1, :]
                higher.append(total)
            return higher[0], higher[1]

        for field in range(3):
            real, imaginary = rows_of(field)
            for strip in range(STRIPS):
                at = strip * 24 + field * 8
                cosine = twist[0, strip : strip + 1, :]
                sine = twist[1, strip : strip + 1, :]
                high, low = halves(real * cosine - imaginary * sine)
                left[which, 0, at : at + 8, :] = high
                left[which, 0, low_rows + at : low_rows + at + 8, :] = low
                high, low = halves(-(real * sine + imaginary * cosine))
                left[which, 1, at : at + 8, :] = high
                left[which, 1, low_rows + at : low_rows + at + 8, :] = low

        return 0

    @pl.when(lat == 0)
    def _():
        lax.fori_loop(0, 2, turned, 0)

    load(lat).wait()

    def block_of(block, _):
        first = pl.multiple_of(block * 256, 256)
        columns = pl.ds(first, 256)
        times = functools.partial(jnp.dot, preferred_element_type=jnp.float32)
        result = None
        for trig in (0, 1):
            high = table[lat, 0, trig, :, columns]
            both = times(left[lat, trig], high)
            term = (both[:low_rows] + both[low_rows:]
                    + times(left[lat, trig, :low_rows], table[lat, 1, trig, :, columns]))
            result = term if result is None else result + term
        number = lax.broadcasted_iota(jnp.int32, (24, 256), 1) + first
        for strip in range(STRIPS):
            piece = jnp.where(number + strip * STRIP < circle_whole,
                              result[strip * 24 : strip * 24 + 24], 0.0)
            where = pl.ds(pl.multiple_of(first + strip * STRIP, 256), 256)
            for field, out in enumerate((out_v, out_d, out_h)):
                out[0, :, where] = piece[field * 8 : field * 8 + 8]
        return 0

    lax.fori_loop(0, STRIP // 256, block_of, 0)

    @pl.when(lat == 1)
    def _():
        for copy in passed:
            copy.wait()


def synthesize(lon_counts, lat_order, depth, diagonal, fourier, pair_row, warm_t, warm_s, basis):
    anywhere = pl.BlockSpec(memory_space=pl.ANY)
    scalar = pl.BlockSpec(memory_space=pltpu.SMEM)
    grid_line = pl.BlockSpec((1, 8, LON_PAD), lambda i: (i, 0, 0))
    return pl.pallas_call(
        synthesis_kernel,
        grid=(2,),
        out_shape=[jax.ShapeDtypeStruct((2, 8, LON_PAD), jnp.float32)] * 5,
        in_specs=[scalar] * 4 + [anywhere] * 5,
        out_specs=[grid_line, grid_line, anywhere, anywhere, grid_line],
        scratch_shapes=[
            pltpu.VMEM((2, 2, 2, WAVES, STRIP), jnp.bfloat16),
            pltpu.VMEM((2, 2, STRIPS * 48, WAVES), jnp.bfloat16),
            pltpu.VMEM((2, 8, WAVES), jnp.float32),
            pltpu.VMEM((6, 8, WAVES), jnp.float32),
            pltpu.VMEM((3, 4, 640), jnp.float32),
            pltpu.VMEM((2, PEERS * 40, 128), jnp.float32),
            pltpu.VMEM((8, 640), jnp.float32),
            pltpu.SemaphoreType.DMA((6,)),
        ],
        compiler_params=pltpu.CompilerParams(vmem_limit_bytes=60 * 2**20),
    )(lon_counts, lat_order, depth, diagonal, fourier, pair_row, warm_t, warm_s, basis)


def body(
    spectral, legendre, pair_list, lon_counts, lat_order, layer_depth_log, diagonal_layer_factor
):
    rows = jnp.transpose(spectral, (0, 2, 1, 3)).reshape(6, 648, 640)
    polynomials = jnp.transpose(legendre, (0, 2, 1))
    fourier, pair_row, warm_t, warm_s, basis = exchange(
        pair_list, lon_counts, lat_order, layer_depth_log, rows, polynomials
    )
    return tuple(
        synthesize(lon_counts, lat_order, layer_depth_log, diagonal_layer_factor, fourier, pair_row,
                   warm_t, warm_s, basis)
    )


def solution(mesh):
    placed = (
        P(None, "lev", "wave", None),
        P("wave", None, None),
        P(),
        P(),
        P(),
        P("lev"),
        P("lev"),
    )
    return jax.shard_map(
        body,
        mesh=mesh,
        in_specs=placed,
        out_specs=(P("wave", "lev", None),) * 5,
        check_vma=False,
    )
```

```python
import functools

import jax
import jax.numpy as jnp
from jax import lax
from jax.experimental import pallas as pl
from jax.experimental.pallas import tpu as pltpu
from jax.sharding import PartitionSpec as P

TRUNC = 1279
ROWS = 1281
LON_PAD = 5376
WAVES = 1280
STRIP = 768
STRIPS = LON_PAD // STRIP
PEERS = 16
SHARE = 40
HALVES = (320, 328)
ORDER = ((2, 2), (1, 0), (3, 0), (0, 1), (0, 3), (1, 2), (3, 2), (2, 1), (2, 3), (2, 0), (0, 2),
         (1, 1), (3, 3), (1, 3), (3, 1))
MESH = pl.DeviceIdType.MESH

COS_TERMS = (1.0, -19.73920440673828, 64.93911743164062, -85.45011138916016,
             60.16740036010742, -25.966703414916992, 6.5273566246032715)
SIN_TERMS = (6.2831854820251465, -41.34170150756836, 81.60513305664062, -76.7030029296875,
             42.02582931518555, -14.899463653564453, 3.2375807762145996)


def turn(product, circle):
    inverse = 1.0 / circle
    part = (product - jnp.floor(product * inverse + 0.5) * circle) * inverse
    square = part * part
    cosine = jnp.full_like(square, COS_TERMS[-1])
    sine = jnp.full_like(square, SIN_TERMS[-1])
    for term in COS_TERMS[-2::-1]:
        cosine = cosine * square + term
    for term in SIN_TERMS[-2::-1]:
        sine = sine * square + term
    return cosine, sine * part


def halves(value):
    high = value.astype(jnp.bfloat16)
    return high, (value - high.astype(jnp.float32)).astype(jnp.bfloat16)


def exchange_kernel(pairs, lon_counts, lat_order, depth, spectral, legendre,
                    out_fourier, pair_row, warm_t, warm_s, out_basis,
                    spec, legs, send_a, send_b, got_a, got_b, stage, rights, lefts, shuffle,
                    summed, halved, slots, send_f, got_f, send_c, got_c, column, table, coef, twist, left,
                    in_sem, leg_sem, spec_send, spec_recv, spec_own, four_send, four_recv, four_own,
                    lev_send, lev_recv, table_sem):
    wave, lev = lax.axis_index("wave"), lax.axis_index("lev")
    across, along = wave // 4, lax.rem(wave, 4)
    times = functools.partial(jnp.dot, preferred_element_type=jnp.float32)

    loads = []
    for part in (1, 0):
        load = pltpu.make_async_copy(spectral.at[pl.ds(3 * part, 3)], spec.at[pl.ds(3 * part, 3)],
                                     in_sem.at[part])
        load.start()
        loads.append(load)
    leg_load = pltpu.make_async_copy(legendre, legs, leg_sem)
    leg_load.start()

    barrier = pltpu.get_barrier_semaphore()
    for step in range(1, PEERS):
        pl.semaphore_signal(barrier, inc=1, device_id=(lax.rem(wave + step, PEERS), lev),
                            device_id_type=MESH)
        pl.semaphore_signal(barrier, inc=1, device_id=(wave, lax.rem(lev + step, PEERS)),
                            device_id_type=MESH)

    def window(duo):
        return jnp.minimum((80 * duo) // 128, 3) * 128

    def shuffle_rows(owner):
        duo, second = owner // 2, lax.rem(owner, 2)
        lane = lax.broadcasted_iota(jnp.int32, (1, 128), 1)
        side = jnp.where(lane >= 60, 1, 0)
        inner = lane - 60 * side
        third = jnp.where(inner >= 20, 1, 0) + jnp.where(inner >= 40, 1, 0) + jnp.where(inner >= 60, 1, 0)
        source = 80 * duo - window(duo) + 40 * second + 20 * side + inner - 20 * third
        row = lax.broadcasted_iota(jnp.int32, (256, 128), 0)
        lanes = pl.ds(pl.multiple_of(second * 128, 128), 128)
        for place in range(3):
            wanted = jnp.where(third == place, source, -1)
            shuffle[duo, place, :, lanes] = jnp.where(row == wanted, 1.0, 0.0).astype(jnp.bfloat16)

    def shuffled_first(owner):
        duo = owner // 2
        lanes = pl.ds(pl.multiple_of(lax.rem(owner, 2) * 128, 128), 128)
        source = pl.ds(pl.multiple_of(window(duo), 128), 256)
        total = None
        for place in range(3):
            term = times(spec[3 + place, : HALVES[0], source], shuffle[duo, place, :, lanes])
            total = term if total is None else total + term
        send_a[1, owner] = total.astype(jnp.bfloat16)

    def owner_of(x, y):
        return lax.rem(across + x, 4) * 4 + lax.rem(along + y, 4)


    copies = []
    waits = {}
    for part in (1, 0):
        loads[1 - part].wait()
        for half, (rows, send, got) in enumerate(zip(HALVES, (send_a, send_b), (got_a, got_b))):
            first = half * HALVES[0]

            def shuffled(duo, _, part=part, first=first, rows=rows, send=send):
                lanes = pl.ds(pl.multiple_of(window(duo), 128), 256)
                total = times(spec[3 * part, first : first + rows, lanes], shuffle[duo, 0])
                for place in (1, 2):
                    total = total + times(spec[3 * part + place, first : first + rows, lanes],
                                          shuffle[duo, place])
                send[part, 2 * duo] = total[:, :128].astype(jnp.bfloat16)
                send[part, 2 * duo + 1] = total[:, 128:].astype(jnp.bfloat16)
                return 0

            opening = part == 1 and half == 0
            if not opening:
                lax.fori_loop(0, 8, shuffled, 0)
            here = []
            for number, (x, y) in enumerate(ORDER):
                other = owner_of(x, y)
                if opening:
                    shuffle_rows(other)
                    shuffled_first(other)
                    if number == 0:
                        pl.semaphore_wait(barrier, 2 * (PEERS - 1))
                copy = pltpu.make_async_remote_copy(
                    src_ref=send.at[part, other], dst_ref=got.at[part, wave],
                    send_sem=spec_send.at[part, half, number], recv_sem=spec_recv.at[part, half, number],
                    device_id=(other, lev), device_id_type=MESH)
                copy.start()
                here.append(copy)
            if opening:
                shuffle_rows(wave)
                shuffled_first(wave)
            own = pltpu.make_async_copy(send.at[part, wave], got.at[part, wave], spec_own.at[part, half])
            own.start()
            waits[part, half] = (here, own)
            copies += here

    leg_load.wait()

    def masked(place, _):
        boundary = TRUNC + 1 - pairs[wave * SHARE + place]
        values = legs[place].astype(jnp.float32)
        row = lax.broadcasted_iota(jnp.int32, values.shape, 1)
        low = jnp.where(row < boundary, values, 0.0)
        high = jnp.where((row >= boundary) & (row < ROWS), values, 0.0)
        lefts[pl.ds(pl.multiple_of(place * 64, 64), 32), :] = low.astype(jnp.bfloat16)
        lefts[pl.ds(pl.multiple_of(place * 64 + 32, 32), 32), :] = high.astype(jnp.bfloat16)
        return 0

    lax.fori_loop(0, SHARE, masked, 0)
    lane = lax.broadcasted_iota(jnp.int32, (8, 128), 1)
    for tile in range(5):
        def listed(step, values, tile=tile):
            for place in range(8):
                at = step * 8 + place
                values = jnp.where(lane == at, pairs[tile * 128 + at], values)
            return values

        values = lax.fori_loop(0, 16, listed, jnp.zeros((8, 128), jnp.int32)).astype(jnp.float32)
        pair_row[:, tile * 128 : tile * 128 + 128] = values
        column[tile * 128 : tile * 128 + 128, :] = jnp.transpose(jnp.broadcast_to(values[:1], (128, 128)))
    row = lax.broadcasted_iota(jnp.int32, (64, 64), 0)
    spot = lax.broadcasted_iota(jnp.int32, (64, 64), 1)
    wanted = jnp.zeros((64, 64), jnp.int32)
    for number in range(32):
        here = (row % 16 == number // 2) & (row // 32 == number % 2)
        wanted = jnp.where(here, lat_order[number], wanted)
    wanted = wanted + 32 * ((row // 16) % 2)
    slots[...] = jnp.where(spot == wanted, 1.0, 0.0).astype(jnp.bfloat16)
    send_f[...] = jnp.zeros_like(send_f)

    def circle_of(lat):
        whole = lon_counts[lat_order[2 * wave + lat]]
        return whole, jnp.full((1, 1), whole, jnp.int32).astype(jnp.float32)

    def table_copy(lat):
        return pltpu.make_async_copy(table.at[lat], out_basis.at[lat], table_sem.at[lat])

    def tables(lat):
        _, circle = circle_of(lat)

        def rows_of(step, _):
            rows = pl.ds(pl.multiple_of(step * 16, 16), 16)
            mirrored = pl.ds(pl.multiple_of(step * 16 + 640, 16), 16)
            strip = lax.broadcasted_iota(jnp.int32, (16, STRIP), 1).astype(jnp.float32)
            number = jnp.concatenate([column[rows, :]] * (STRIP // 128), axis=1)
            for where, value in ((rows, number), (mirrored, TRUNC - number)):
                cosine, sine = turn(value * strip, circle)
                table[lat, 0, 0, where, :], table[lat, 1, 0, where, :] = halves(cosine)
                table[lat, 0, 1, where, :], table[lat, 1, 1, where, :] = halves(sine)
            return 0

        lax.fori_loop(0, 40, rows_of, 0)
        table_copy(lat).start()

    def twists(lat):
        _, circle = circle_of(lat)
        pair = pair_row[:1, :]
        number = jnp.concatenate([pair, TRUNC - pair], axis=1)
        weight = jnp.where(2.0 * number < circle, jnp.where(number == 0.0, 1.0, 2.0), 0.0)
        start = (lax.broadcasted_iota(jnp.int32, (8, WAVES), 0) * STRIP).astype(jnp.float32)
        cosine, sine = turn(start * number, circle)
        twist[lat, 0] = cosine * weight
        twist[lat, 1] = sine * weight

    def legendre_sums(part):
        for half in (0, 1):
            here, own = waits[part, half]
            for copy in here:
                copy.wait_recv()
            own.wait()

        def widen(source, _):
            stage[pl.ds(pl.multiple_of(source * 648, 8), 320), :] = got_a[part, source].astype(jnp.float32)
            stage[pl.ds(pl.multiple_of(source * 648 + 320, 8), 328), :] = got_b[part, source].astype(jnp.float32)
            return 0

        lax.fori_loop(0, PEERS, widen, 0)

        def gather(chunk, _):
            rows = pl.ds(pl.multiple_of(chunk * 144, 16), 144)
            for duo in range(4):
                even = stage[pl.ds(chunk * 1152 + 2 * duo, 144, stride=8), :]
                odd = stage[pl.ds(chunk * 1152 + 2 * duo + 1, 144, stride=8), :]
                lower = jnp.where(left_lane, even, pltpu.roll(odd, 64, 1))
                upper = jnp.where(left_lane, pltpu.roll(even, 68, 1), pltpu.roll(odd, 4, 1))
                lanes = slice(128 * (duo % 2), 128 * (duo % 2) + 128)
                rights[duo // 2, rows, lanes] = lower.astype(jnp.bfloat16)
                rights[2 + duo // 2, rows, lanes] = upper.astype(jnp.bfloat16)
            return 0

        left_lane = lax.broadcasted_iota(jnp.int32, (1, 128), 1) < 64
        lax.fori_loop(0, 9, gather, 0)
        inner = lax.broadcasted_iota(jnp.int32, (1, 256), 1)
        for step in (128, 64, 40, 20):
            inner = jnp.where(inner >= step, inner - step, inner)

        def levels(block, _):
            side = block // 2

            def group(chunk, total):
                first = pl.multiple_of(side * 1280 + chunk * 640, 128)
                result = times(lefts[pl.ds(first, 640), :], rights[block])
                for place in range(10):
                    total = total + jnp.where(inner == chunk * 10 + place,
                                              result[place * 64 : place * 64 + 64], 0.0)
                return total

            total = lax.fori_loop(0, 2, group, jnp.zeros((64, 256), jnp.float32))
            halved[block] = total
            return 0

        lax.fori_loop(0, 4, levels, 0)
        for duo in range(4):
            lanes = slice(128 * (duo % 2), 128 * (duo % 2) + 128)
            lower, upper = halved[duo // 2, :, lanes], halved[2 + duo // 2, :, lanes]
            summed[duo, :, :128] = jnp.where(left_lane, lower, pltpu.roll(upper, 64, 1))
            summed[duo, :, 128:] = jnp.where(left_lane, pltpu.roll(lower, 64, 1), upper)

    def in_order(rest):
        moved = jnp.zeros(rest.shape, jnp.float32)
        for _ in range(3):
            piece = rest.astype(jnp.bfloat16)
            rest = rest - piece.astype(jnp.float32)
            moved = moved + times(slots[...], piece)
        return moved

    def send_fourier(part):
        for duo in range(4):
            moved = in_order(summed[duo])
            for place in range(4):
                for odd in (0, 1):
                    send_f[part, pl.ds(8 * place + 2 * duo + odd, 16, stride=40), :] = (
                        moved[16 * place : 16 * place + 16, 128 * odd : 128 * odd + 128])
        here = []
        for number, (x, y) in enumerate(ORDER):
            other = lax.rem(across + x, 4) * 4 + lax.rem(along + y, 4)
            copy = pltpu.make_async_remote_copy(
                src_ref=send_f.at[part, pl.ds(pl.multiple_of(other * 40, 8), 40), :],
                dst_ref=got_f.at[part, pl.ds(pl.multiple_of(wave * 40, 8), 40), :],
                send_sem=four_send.at[part, number], recv_sem=four_recv.at[part, number],
                device_id=(other, lev), device_id_type=MESH)
            copy.start()
            here.append(copy)
        own = pltpu.make_async_copy(
            send_f.at[part, pl.ds(pl.multiple_of(wave * 40, 8), 40), :],
            got_f.at[part, pl.ds(pl.multiple_of(wave * 40, 8), 40), :], four_own.at[part])
        own.start()
        copies.extend(here)
        return here, own

    def arrived(here, own):
        for copy in here:
            copy.wait_recv()
        own.wait()

    line = lax.broadcasted_iota(jnp.int32, (1, 128), 1)

    def spread(take, keep, height):
        for place in range(3):
            tiles = [jnp.zeros((height, 128), jnp.float32)] * 5
            for source in range(PEERS):
                value = take(source)
                for side in range(2):
                    goal = source * SHARE + 20 * side
                    tile, offset = goal // 128, goal % 128
                    rolled = pltpu.roll(value, (offset - place * 20 - 64 * side) % 128, 1)
                    end = offset + 20
                    tiles[tile] = jnp.where((line >= offset) & (line < end), rolled, tiles[tile])
                    if end > 128:
                        tiles[tile + 1] = jnp.where(line < end - 128, rolled, tiles[tile + 1])
            for tile in range(5):
                keep(place, tile, tiles[tile])

    def warm(lat, _):
        for side in range(2):
            def take(source, side=side):
                return got_f[1, pl.ds(pl.multiple_of(source * 40 + lat * 16 + side * 8, 8), 8), :]

            def keep(place, tile, value, side=side):
                at = side * 640 + tile * 128
                coef[place, :, at : at + 128] = value

            spread(take, keep, 8)
        pair = pair_row[:1, :]
        factor = jnp.concatenate([pair, TRUNC - pair], axis=1) * (1.0 / (TRUNC + 1))
        low_rows = STRIPS * 16
        for order in range(2):
            real, imaginary = coef[1], coef[2]
            if order == 1:
                real, imaginary = -factor * imaginary, factor * real
            for strip in range(STRIPS):
                at = strip * 16 + order * 8
                cosine = twist[lat, 0, strip : strip + 1, :]
                sine = twist[lat, 1, strip : strip + 1, :]
                high, low = halves(real * cosine - imaginary * sine)
                left[0, at : at + 8, :] = high
                left[0, low_rows + at : low_rows + at + 8, :] = low
                high, low = halves(-(real * sine + imaginary * cosine))
                left[1, at : at + 8, :] = high
                left[1, low_rows + at : low_rows + at + 8, :] = low
        whole, _ = circle_of(lat)

        def block_of(block, _):
            first = pl.multiple_of(block * 256, 256)
            columns = pl.ds(first, 256)
            result = None
            for trig in (0, 1):
                both = times(left[trig], table[lat, 0, trig, :, columns])
                term = (both[:low_rows] + both[low_rows:]
                        + times(left[trig, :low_rows], table[lat, 1, trig, :, columns]))
                result = term if result is None else result + term
            number = lax.broadcasted_iota(jnp.int32, (16, 256), 1) + first
            for strip in range(STRIPS):
                piece = jnp.where(number + strip * STRIP < whole, result[strip * 16 : strip * 16 + 16], 0.0)
                where = pl.ds(pl.multiple_of(first + strip * STRIP, 256), 256)
                warm_t[lat, :, where] = piece[:8]
                warm_s[lat, :, where] = piece[8:]
            return 0

        lax.fori_loop(0, STRIP // 256, block_of, 0)
        return 0

    for lat in range(2):
        twists(lat)
        tables(lat)
    legendre_sums(1)
    lower = jnp.zeros((64, 128), jnp.float32)
    for duo in range(4):
        lower = lower + depth[2 * duo] * summed[duo, :, :128] + depth[2 * duo + 1] * summed[duo, :, 128:]
    send_c[...] = lower
    lev_copies = []
    for step in range(1, PEERS):
        copy = pltpu.make_async_remote_copy(
            src_ref=send_c, dst_ref=got_c.at[lev],
            send_sem=lev_send.at[step - 1], recv_sem=lev_recv.at[step - 1],
            device_id=(wave, lax.rem(lev + step, PEERS)), device_id_type=MESH)
        copy.start()
        lev_copies.append(copy)
    first = send_fourier(1)
    legendre_sums(0)
    for copy in lev_copies:
        copy.wait_recv()
    above = jnp.zeros((64, 128), jnp.float32)
    got_c[lev] = send_c[...]
    for other in range(PEERS):
        above = above + jnp.where(other > lev, got_c[other], 0.0)
    above = in_order(above)
    for place in range(4):
        send_f[0, pl.ds(32 + place, 16, stride=40), :] = above[16 * place : 16 * place + 16]
    second = send_fourier(0)
    arrived(*first)
    lax.fori_loop(0, 2, warm, 0)
    arrived(*second)
    out_fourier[...] = got_f[...]
    for copy in copies + lev_copies:
        copy.wait_send()
    table_copy(0).wait()
    table_copy(1).wait()


def exchange(pairs, lon_counts, lat_order, depth, spectral, legendre):
    anywhere = pl.BlockSpec(memory_space=pl.ANY)
    vector = pl.BlockSpec(memory_space=pltpu.VMEM)
    scalar = pl.BlockSpec(memory_space=pltpu.SMEM)
    dma = pltpu.SemaphoreType.DMA
    return pl.pallas_call(
        exchange_kernel,
        out_shape=[
            jax.ShapeDtypeStruct((2, PEERS * 40, 128), jnp.float32),
            jax.ShapeDtypeStruct((8, 640), jnp.float32),
            jax.ShapeDtypeStruct((2, 8, LON_PAD), jnp.float32),
            jax.ShapeDtypeStruct((2, 8, LON_PAD), jnp.float32),
            jax.ShapeDtypeStruct((2, 2, 2, WAVES, STRIP), jnp.bfloat16),
        ],
        in_specs=[scalar] * 4 + [anywhere] * 2,
        out_specs=[vector] * 4 + [anywhere],
        scratch_shapes=[
            pltpu.VMEM((6, 648, 640), jnp.bfloat16),
            pltpu.VMEM((SHARE, 32, 1296), jnp.bfloat16),
            pltpu.VMEM((2, PEERS, HALVES[0], 128), jnp.bfloat16),
            pltpu.VMEM((2, PEERS, HALVES[1], 128), jnp.bfloat16),
            pltpu.VMEM((2, PEERS, HALVES[0], 128), jnp.bfloat16),
            pltpu.VMEM((2, PEERS, HALVES[1], 128), jnp.bfloat16),
            pltpu.VMEM((PEERS * 648, 128), jnp.float32),
            pltpu.VMEM((4, 1296, 256), jnp.bfloat16),
            pltpu.VMEM((SHARE * 64, 1296), jnp.bfloat16),
            pltpu.VMEM((8, 3, 256, 256), jnp.bfloat16),
            pltpu.VMEM((4, 64, 256), jnp.float32),
            pltpu.VMEM((4, 64, 256), jnp.float32),
            pltpu.VMEM((64, 64), jnp.bfloat16),
            pltpu.VMEM((2, PEERS * 40, 128), jnp.float32),
            pltpu.VMEM((2, PEERS * 40, 128), jnp.float32),
            pltpu.VMEM((64, 128), jnp.float32),
            pltpu.VMEM((PEERS, 64, 128), jnp.float32),
            pltpu.VMEM((640, 128), jnp.float32),
            pltpu.VMEM((2, 2, 2, WAVES, STRIP), jnp.bfloat16),
            pltpu.VMEM((3, 8, WAVES), jnp.float32),
            pltpu.VMEM((2, 2, 8, WAVES), jnp.float32),
            pltpu.VMEM((2, STRIPS * 32, WAVES), jnp.bfloat16),
            dma((2,)), dma, dma((2, 2, 15)), dma((2, 2, 15)), dma((2, 2)),
            dma((2, 15)), dma((2, 15)), dma((2,)), dma((15,)), dma((15,)), dma((2,)),
        ],
        compiler_params=pltpu.CompilerParams(
            collective_id=0, has_side_effects=True, vmem_limit_bytes=60 * 2**20
        ),
    )(pairs, lon_counts, lat_order, depth, spectral, legendre)


def synthesis_kernel(lon_counts, lat_order, depth, diagonal, fourier_far, pair_far, warm_t, warm_s, basis,
                     out_v, out_d, out_t, out_s, out_h,
                     table, left, twist, coef, upper, fourier, pair_row, near_t, near_s, table_sem):
    lat = pl.program_id(0)
    wave_group = lax.axis_index("wave")

    def load(which):
        return pltpu.make_async_copy(basis.at[which], table.at[which], table_sem.at[which])

    passed = (pltpu.make_async_copy(warm_t, near_t, table_sem.at[4]),
              pltpu.make_async_copy(warm_s, near_s, table_sem.at[5]))

    @pl.when(lat == 0)
    def _():
        near = (pltpu.make_async_copy(pair_far, pair_row, table_sem.at[2]),
                pltpu.make_async_copy(fourier_far, fourier, table_sem.at[3]))
        for copy in near:
            copy.start()
        load(0).start()
        load(1).start()
        for copy in passed:
            copy.start()
        for copy in near:
            copy.wait()

    circle_whole = lon_counts[lat_order[2 * wave_group + lat]]
    low_rows = STRIPS * 24
    lane = lax.broadcasted_iota(jnp.int32, (1, 128), 1)

    def spread(take, keep, height):
        for place in range(3):
            tiles = [jnp.zeros((height, 128), jnp.float32)] * 5
            for source in range(PEERS):
                value = take(source)
                for side in range(2):
                    goal = source * SHARE + 20 * side
                    tile, offset = goal // 128, goal % 128
                    rolled = pltpu.roll(value, (offset - place * 20 - 64 * side) % 128, 1)
                    end = offset + 20
                    tiles[tile] = jnp.where((lane >= offset) & (lane < end), rolled, tiles[tile])
                    if end > 128:
                        tiles[tile + 1] = jnp.where(lane < end - 128, rolled, tiles[tile + 1])
            for tile in range(5):
                keep(place, tile, tiles[tile])

    def turned(which, _):
        count = lon_counts[lat_order[2 * wave_group + which]]
        circle = jnp.full((1, 1), count, jnp.int32).astype(jnp.float32)
        for part in range(2):
            for side in range(2):
                def take(source, part=part, side=side):
                    return fourier[part, pl.ds(pl.multiple_of(source * 40 + which * 16 + side * 8, 8), 8), :]

                def keep(place, tile, value, part=part, side=side):
                    at = side * 640 + tile * 128
                    coef[3 * part + place, :, at : at + 128] = value

                spread(take, keep, 8)

        def take_above(source):
            return fourier[0, source * 40 + 32 : source * 40 + 36, :]

        def keep_above(place, tile, value):
            upper[place, :, tile * 128 : tile * 128 + 128] = value

        spread(take_above, keep_above, 4)

        pair = pair_row[:1, :]
        wave = jnp.concatenate([pair, TRUNC - pair], axis=1)
        weight = jnp.where(2.0 * wave < circle, jnp.where(wave == 0.0, 1.0, 2.0), 0.0)
        start = (lax.broadcasted_iota(jnp.int32, (8, WAVES), 0) * STRIP).astype(jnp.float32)
        cosine, sine = turn(start * wave, circle)
        twist[0] = cosine * weight
        twist[1] = sine * weight
        level_of = lax.broadcasted_iota(jnp.int32, (8, 1), 0)

        def rows_of(field):
            if field < 2:
                return coef[2 * field], coef[2 * field + 1]
            real, imaginary = coef[4], coef[5]
            higher = []
            for value, place in ((real, 1), (imaginary, 2)):
                total = jnp.broadcast_to(
                    jnp.concatenate([upper[place, pl.ds(2 * which, 1), :], upper[place, pl.ds(2 * which + 1, 1), :]], axis=1),
                    (8, WAVES))
                for level in range(8):
                    share = jnp.where(level_of == level, diagonal[level],
                                      jnp.where(level_of < level, depth[level], 0.0))
                    total = total + share * value[level : level + 1, :]
                higher.append(total)
            return higher[0], higher[1]

        for field in range(3):
            real, imaginary = rows_of(field)
            for strip in range(STRIPS):
                at = strip * 24 + field * 8
                cosine = twist[0, strip : strip + 1, :]
                sine = twist[1, strip : strip + 1, :]
                high, low = halves(real * cosine - imaginary * sine)
                left[which, 0, at : at + 8, :] = high
                left[which, 0, low_rows + at : low_rows + at + 8, :] = low
                high, low = halves(-(real * sine + imaginary * cosine))
                left[which, 1, at : at + 8, :] = high
                left[which, 1, low_rows + at : low_rows + at + 8, :] = low

        return 0

    @pl.when(lat == 0)
    def _():
        lax.fori_loop(0, 2, turned, 0)

    load(lat).wait()

    def block_of(block, _):
        first = pl.multiple_of(block * 256, 256)
        columns = pl.ds(first, 256)
        times = functools.partial(jnp.dot, preferred_element_type=jnp.float32)
        result = None
        for trig in (0, 1):
            high = table[lat, 0, trig, :, columns]
            both = times(left[lat, trig], high)
            term = (both[:low_rows] + both[low_rows:]
                    + times(left[lat, trig, :low_rows], table[lat, 1, trig, :, columns]))
            result = term if result is None else result + term
        number = lax.broadcasted_iota(jnp.int32, (24, 256), 1) + first
        for strip in range(STRIPS):
            piece = jnp.where(number + strip * STRIP < circle_whole,
                              result[strip * 24 : strip * 24 + 24], 0.0)
            where = pl.ds(pl.multiple_of(first + strip * STRIP, 256), 256)
            for field, out in enumerate((out_v, out_d, out_h)):
                out[0, :, where] = piece[field * 8 : field * 8 + 8]
        return 0

    lax.fori_loop(0, STRIP // 256, block_of, 0)

    @pl.when(lat == 0)
    def _():
        for copy in passed:
            copy.wait()

    out_t[0] = near_t[lat]
    out_s[0] = near_s[lat]


def synthesize(lon_counts, lat_order, depth, diagonal, fourier, pair_row, warm_t, warm_s, basis):
    anywhere = pl.BlockSpec(memory_space=pl.ANY)
    scalar = pl.BlockSpec(memory_space=pltpu.SMEM)
    grid_line = pl.BlockSpec((1, 8, LON_PAD), lambda i: (i, 0, 0))
    return pl.pallas_call(
        synthesis_kernel,
        grid=(2,),
        out_shape=[jax.ShapeDtypeStruct((2, 8, LON_PAD), jnp.float32)] * 5,
        in_specs=[scalar] * 4 + [anywhere] * 5,
        out_specs=[grid_line] * 5,
        scratch_shapes=[
            pltpu.VMEM((2, 2, 2, WAVES, STRIP), jnp.bfloat16),
            pltpu.VMEM((2, 2, STRIPS * 48, WAVES), jnp.bfloat16),
            pltpu.VMEM((2, 8, WAVES), jnp.float32),
            pltpu.VMEM((6, 8, WAVES), jnp.float32),
            pltpu.VMEM((3, 4, 640), jnp.float32),
            pltpu.VMEM((2, PEERS * 40, 128), jnp.float32),
            pltpu.VMEM((8, 640), jnp.float32),
            pltpu.VMEM((2, 8, LON_PAD), jnp.float32),
            pltpu.VMEM((2, 8, LON_PAD), jnp.float32),
            pltpu.SemaphoreType.DMA((6,)),
        ],
        compiler_params=pltpu.CompilerParams(vmem_limit_bytes=60 * 2**20),
    )(lon_counts, lat_order, depth, diagonal, fourier, pair_row, warm_t, warm_s, basis)


def body(
    spectral, legendre, pair_list, lon_counts, lat_order, layer_depth_log, diagonal_layer_factor
):
    rows = jnp.transpose(spectral, (0, 2, 1, 3)).reshape(6, 648, 640)
    polynomials = jnp.transpose(legendre, (0, 2, 1))
    fourier, pair_row, warm_t, warm_s, basis = exchange(
        pair_list, lon_counts, lat_order, layer_depth_log, rows, polynomials
    )
    return tuple(
        synthesize(lon_counts, lat_order, layer_depth_log, diagonal_layer_factor, fourier, pair_row,
                   warm_t, warm_s, basis)
    )


def solution(mesh):
    placed = (
        P(None, "lev", "wave", None),
        P("wave", None, None),
        P(),
        P(),
        P(),
        P("lev"),
        P("lev"),
    )
    return jax.shard_map(
        body,
        mesh=mesh,
        in_specs=placed,
        out_specs=(P("wave", "lev", None),) * 5,
        check_vma=False,
    )
```

```python
import functools

import jax
import jax.numpy as jnp
from jax import lax
from jax.experimental import pallas as pl
from jax.experimental.pallas import tpu as pltpu
from jax.sharding import PartitionSpec as P

TRUNC = 1279
ROWS = 1281
LON_PAD = 5376
WAVES = 1280
STRIP = 768
STRIPS = LON_PAD // STRIP
PEERS = 16
SHARE = 40
THIRDS = (208, 208, 232)
ORDER = ((2, 2), (1, 0), (3, 0), (0, 1), (0, 3), (1, 2), (3, 2), (2, 1), (2, 3), (2, 0), (0, 2),
         (1, 1), (3, 3), (1, 3), (3, 1))
MESH = pl.DeviceIdType.MESH

COS_TERMS = (1.0, -19.73920440673828, 64.93911743164062, -85.45011138916016,
             60.16740036010742, -25.966703414916992, 6.5273566246032715)
SIN_TERMS = (6.2831854820251465, -41.34170150756836, 81.60513305664062, -76.7030029296875,
             42.02582931518555, -14.899463653564453, 3.2375807762145996)


def turn(product, circle):
    inverse = 1.0 / circle
    part = (product - jnp.floor(product * inverse + 0.5) * circle) * inverse
    square = part * part
    cosine = jnp.full_like(square, COS_TERMS[-1])
    sine = jnp.full_like(square, SIN_TERMS[-1])
    for term in COS_TERMS[-2::-1]:
        cosine = cosine * square + term
    for term in SIN_TERMS[-2::-1]:
        sine = sine * square + term
    return cosine, sine * part


def halves(value):
    high = value.astype(jnp.bfloat16)
    return high, (value - high.astype(jnp.float32)).astype(jnp.bfloat16)


def exchange_kernel(pairs, lon_counts, lat_order, depth, spectral, legendre,
                    out_fourier, pair_row, warm_t, warm_s, out_basis,
                    spec, legs, send_a, send_b, send_c3, got_a, got_b, got_c3, stage, rights, lefts, shuffle,
                    summed, halved, slots, send_f, got_f, send_c, got_c, column, table, coef, twist, left,
                    in_sem, leg_sem, spec_send, spec_recv, spec_own, four_send, four_recv, four_own,
                    lev_send, lev_recv, table_sem):
    wave, lev = lax.axis_index("wave"), lax.axis_index("lev")
    across, along = wave // 4, lax.rem(wave, 4)
    times = functools.partial(jnp.dot, preferred_element_type=jnp.float32)

    loads = []
    for part in (1, 0):
        load = pltpu.make_async_copy(spectral.at[pl.ds(3 * part, 3)], spec.at[pl.ds(3 * part, 3)],
                                     in_sem.at[part])
        load.start()
        loads.append(load)
    leg_load = pltpu.make_async_copy(legendre, legs, leg_sem)
    leg_load.start()

    barrier = pltpu.get_barrier_semaphore()
    for step in range(1, PEERS):
        pl.semaphore_signal(barrier, inc=1, device_id=(lax.rem(wave + step, PEERS), lev),
                            device_id_type=MESH)
        pl.semaphore_signal(barrier, inc=1, device_id=(wave, lax.rem(lev + step, PEERS)),
                            device_id_type=MESH)

    def window(duo):
        return jnp.minimum((80 * duo) // 128, 3) * 128

    def shuffle_rows(owner):
        duo, second = owner // 2, lax.rem(owner, 2)
        lane = lax.broadcasted_iota(jnp.int32, (1, 128), 1)
        side = jnp.where(lane >= 60, 1, 0)
        inner = lane - 60 * side
        third = jnp.where(inner >= 20, 1, 0) + jnp.where(inner >= 40, 1, 0) + jnp.where(inner >= 60, 1, 0)
        source = 80 * duo - window(duo) + 40 * second + 20 * side + inner - 20 * third
        row = lax.broadcasted_iota(jnp.int32, (256, 128), 0)
        lanes = pl.ds(pl.multiple_of(second * 128, 128), 128)
        for place in range(3):
            wanted = jnp.where(third == place, source, -1)
            shuffle[duo, place, :, lanes] = jnp.where(row == wanted, 1.0, 0.0).astype(jnp.bfloat16)

    def shuffled_first(owner):
        duo = owner // 2
        lanes = pl.ds(pl.multiple_of(lax.rem(owner, 2) * 128, 128), 128)
        source = pl.ds(pl.multiple_of(window(duo), 128), 256)
        total = None
        for place in range(3):
            term = times(spec[3 + place, : THIRDS[0], source], shuffle[duo, place, :, lanes])
            total = term if total is None else total + term
        send_a[1, owner] = total.astype(jnp.bfloat16)

    def owner_of(x, y):
        return lax.rem(across + x, 4) * 4 + lax.rem(along + y, 4)


    copies = []
    waits = {}
    for part in (1, 0):
        loads[1 - part].wait()
        for half, (rows, send, got) in enumerate(zip(THIRDS, (send_a, send_b, send_c3), (got_a, got_b, got_c3))):
            first = half * THIRDS[0]

            def shuffled(duo, _, part=part, first=first, rows=rows, send=send):
                lanes = pl.ds(pl.multiple_of(window(duo), 128), 256)
                total = times(spec[3 * part, first : first + rows, lanes], shuffle[duo, 0])
                for place in (1, 2):
                    total = total + times(spec[3 * part + place, first : first + rows, lanes],
                                          shuffle[duo, place])
                send[part, 2 * duo] = total[:, :128].astype(jnp.bfloat16)
                send[part, 2 * duo + 1] = total[:, 128:].astype(jnp.bfloat16)
                return 0

            opening = part == 1 and half == 0
            if not opening:
                lax.fori_loop(0, 8, shuffled, 0)
            here = []
            for number, (x, y) in enumerate(ORDER):
                other = owner_of(x, y)
                if opening:
                    shuffle_rows(other)
                    shuffled_first(other)
                    if number == 0:
                        pl.semaphore_wait(barrier, 2 * (PEERS - 1))
                copy = pltpu.make_async_remote_copy(
                    src_ref=send.at[part, other], dst_ref=got.at[part, wave],
                    send_sem=spec_send.at[part, half, number], recv_sem=spec_recv.at[part, half, number],
                    device_id=(other, lev), device_id_type=MESH)
                copy.start()
                here.append(copy)
            if opening:
                shuffle_rows(wave)
                shuffled_first(wave)
            own = pltpu.make_async_copy(send.at[part, wave], got.at[part, wave], spec_own.at[part, half])
            own.start()
            waits[part, half] = (here, own)
            copies += here

    leg_load.wait()

    def masked(place, _):
        boundary = TRUNC + 1 - pairs[wave * SHARE + place]
        values = legs[place].astype(jnp.float32)
        row = lax.broadcasted_iota(jnp.int32, values.shape, 1)
        low = jnp.where(row < boundary, values, 0.0)
        high = jnp.where((row >= boundary) & (row < ROWS), values, 0.0)
        lefts[pl.ds(pl.multiple_of(place * 64, 64), 32), :] = low.astype(jnp.bfloat16)
        lefts[pl.ds(pl.multiple_of(place * 64 + 32, 32), 32), :] = high.astype(jnp.bfloat16)
        return 0

    lax.fori_loop(0, SHARE, masked, 0)
    lane = lax.broadcasted_iota(jnp.int32, (8, 128), 1)
    for tile in range(5):
        def listed(step, values, tile=tile):
            for place in range(8):
                at = step * 8 + place
                values = jnp.where(lane == at, pairs[tile * 128 + at], values)
            return values

        values = lax.fori_loop(0, 16, listed, jnp.zeros((8, 128), jnp.int32)).astype(jnp.float32)
        pair_row[:, tile * 128 : tile * 128 + 128] = values
        column[tile * 128 : tile * 128 + 128, :] = jnp.transpose(jnp.broadcast_to(values[:1], (128, 128)))
    row = lax.broadcasted_iota(jnp.int32, (64, 64), 0)
    spot = lax.broadcasted_iota(jnp.int32, (64, 64), 1)
    wanted = jnp.zeros((64, 64), jnp.int32)
    for number in range(32):
        here = (row % 16 == number // 2) & (row // 32 == number % 2)
        wanted = jnp.where(here, lat_order[number], wanted)
    wanted = wanted + 32 * ((row // 16) % 2)
    slots[...] = jnp.where(spot == wanted, 1.0, 0.0).astype(jnp.bfloat16)
    send_f[...] = jnp.zeros_like(send_f)

    def circle_of(lat):
        whole = lon_counts[lat_order[2 * wave + lat]]
        return whole, jnp.full((1, 1), whole, jnp.int32).astype(jnp.float32)

    def table_copy(lat):
        return pltpu.make_async_copy(table.at[lat], out_basis.at[lat], table_sem.at[lat])

    def tables(lat):
        _, circle = circle_of(lat)

        def rows_of(step, _):
            rows = pl.ds(pl.multiple_of(step * 16, 16), 16)
            mirrored = pl.ds(pl.multiple_of(step * 16 + 640, 16), 16)
            strip = lax.broadcasted_iota(jnp.int32, (16, STRIP), 1).astype(jnp.float32)
            number = jnp.concatenate([column[rows, :]] * (STRIP // 128), axis=1)
            for where, value in ((rows, number), (mirrored, TRUNC - number)):
                cosine, sine = turn(value * strip, circle)
                table[lat, 0, 0, where, :], table[lat, 1, 0, where, :] = halves(cosine)
                table[lat, 0, 1, where, :], table[lat, 1, 1, where, :] = halves(sine)
            return 0

        lax.fori_loop(0, 40, rows_of, 0)
        table_copy(lat).start()

    def twists(lat):
        _, circle = circle_of(lat)
        pair = pair_row[:1, :]
        number = jnp.concatenate([pair, TRUNC - pair], axis=1)
        weight = jnp.where(2.0 * number < circle, jnp.where(number == 0.0, 1.0, 2.0), 0.0)
        start = (lax.broadcasted_iota(jnp.int32, (8, WAVES), 0) * STRIP).astype(jnp.float32)
        cosine, sine = turn(start * number, circle)
        twist[lat, 0] = cosine * weight
        twist[lat, 1] = sine * weight

    def legendre_sums(part):
        for half, (rows, got) in enumerate(zip(THIRDS, (got_a, got_b, got_c3))):
            here, own = waits[part, half]
            for copy in here:
                copy.wait_recv()
            own.wait()

            def widen(source, _, rows=rows, got=got, first=half * THIRDS[0]):
                stage[pl.ds(pl.multiple_of(source * 648 + first, 8), rows), :] = got[part, source].astype(jnp.float32)
                return 0

            lax.fori_loop(0, PEERS, widen, 0)

        def gather(chunk, _):
            rows = pl.ds(pl.multiple_of(chunk * 144, 16), 144)
            for duo in range(4):
                even = stage[pl.ds(chunk * 1152 + 2 * duo, 144, stride=8), :]
                odd = stage[pl.ds(chunk * 1152 + 2 * duo + 1, 144, stride=8), :]
                lower = jnp.where(left_lane, even, pltpu.roll(odd, 64, 1))
                upper = jnp.where(left_lane, pltpu.roll(even, 68, 1), pltpu.roll(odd, 4, 1))
                lanes = slice(128 * (duo % 2), 128 * (duo % 2) + 128)
                rights[duo // 2, rows, lanes] = lower.astype(jnp.bfloat16)
                rights[2 + duo // 2, rows, lanes] = upper.astype(jnp.bfloat16)
            return 0

        left_lane = lax.broadcasted_iota(jnp.int32, (1, 128), 1) < 64
        lax.fori_loop(0, 9, gather, 0)
        inner = lax.broadcasted_iota(jnp.int32, (1, 256), 1)
        for step in (128, 64, 40, 20):
            inner = jnp.where(inner >= step, inner - step, inner)

        def levels(block, _):
            side = block // 2

            def group(chunk, total):
                first = pl.multiple_of(side * 1280 + chunk * 640, 128)
                result = times(lefts[pl.ds(first, 640), :], rights[block])
                for place in range(10):
                    total = total + jnp.where(inner == chunk * 10 + place,
                                              result[place * 64 : place * 64 + 64], 0.0)
                return total

            total = lax.fori_loop(0, 2, group, jnp.zeros((64, 256), jnp.float32))
            halved[block] = total
            return 0

        lax.fori_loop(0, 4, levels, 0)
        for duo in range(4):
            lanes = slice(128 * (duo % 2), 128 * (duo % 2) + 128)
            lower, upper = halved[duo // 2, :, lanes], halved[2 + duo // 2, :, lanes]
            summed[duo, :, :128] = jnp.where(left_lane, lower, pltpu.roll(upper, 64, 1))
            summed[duo, :, 128:] = jnp.where(left_lane, pltpu.roll(lower, 64, 1), upper)

    def in_order(rest):
        moved = jnp.zeros(rest.shape, jnp.float32)
        for _ in range(3):
            piece = rest.astype(jnp.bfloat16)
            rest = rest - piece.astype(jnp.float32)
            moved = moved + times(slots[...], piece)
        return moved

    def send_fourier(part):
        for duo in range(4):
            moved = in_order(summed[duo])
            for place in range(4):
                for odd in (0, 1):
                    send_f[part, pl.ds(8 * place + 2 * duo + odd, 16, stride=40), :] = (
                        moved[16 * place : 16 * place + 16, 128 * odd : 128 * odd + 128])
        here = []
        for number, (x, y) in enumerate(ORDER):
            other = lax.rem(across + x, 4) * 4 + lax.rem(along + y, 4)
            copy = pltpu.make_async_remote_copy(
                src_ref=send_f.at[part, pl.ds(pl.multiple_of(other * 40, 8), 40), :],
                dst_ref=got_f.at[part, pl.ds(pl.multiple_of(wave * 40, 8), 40), :],
                send_sem=four_send.at[part, number], recv_sem=four_recv.at[part, number],
                device_id=(other, lev), device_id_type=MESH)
            copy.start()
            here.append(copy)
        own = pltpu.make_async_copy(
            send_f.at[part, pl.ds(pl.multiple_of(wave * 40, 8), 40), :],
            got_f.at[part, pl.ds(pl.multiple_of(wave * 40, 8), 40), :], four_own.at[part])
        own.start()
        copies.extend(here)
        return here, own

    def arrived(here, own):
        for copy in here:
            copy.wait_recv()
        own.wait()

    line = lax.broadcasted_iota(jnp.int32, (1, 128), 1)

    def spread(take, keep, height):
        for place in range(3):
            tiles = [jnp.zeros((height, 128), jnp.float32)] * 5
            for source in range(PEERS):
                value = take(source)
                for side in range(2):
                    goal = source * SHARE + 20 * side
                    tile, offset = goal // 128, goal % 128
                    rolled = pltpu.roll(value, (offset - place * 20 - 64 * side) % 128, 1)
                    end = offset + 20
                    tiles[tile] = jnp.where((line >= offset) & (line < end), rolled, tiles[tile])
                    if end > 128:
                        tiles[tile + 1] = jnp.where(line < end - 128, rolled, tiles[tile + 1])
            for tile in range(5):
                keep(place, tile, tiles[tile])

    def warm(lat, _):
        for side in range(2):
            def take(source, side=side):
                return got_f[1, pl.ds(pl.multiple_of(source * 40 + lat * 16 + side * 8, 8), 8), :]

            def keep(place, tile, value, side=side):
                at = side * 640 + tile * 128
                coef[place, :, at : at + 128] = value

            spread(take, keep, 8)
        pair = pair_row[:1, :]
        factor = jnp.concatenate([pair, TRUNC - pair], axis=1) * (1.0 / (TRUNC + 1))
        low_rows = STRIPS * 16
        for order in range(2):
            real, imaginary = coef[1], coef[2]
            if order == 1:
                real, imaginary = -factor * imaginary, factor * real
            for strip in range(STRIPS):
                at = strip * 16 + order * 8
                cosine = twist[lat, 0, strip : strip + 1, :]
                sine = twist[lat, 1, strip : strip + 1, :]
                high, low = halves(real * cosine - imaginary * sine)
                left[0, at : at + 8, :] = high
                left[0, low_rows + at : low_rows + at + 8, :] = low
                high, low = halves(-(real * sine + imaginary * cosine))
                left[1, at : at + 8, :] = high
                left[1, low_rows + at : low_rows + at + 8, :] = low
        whole, _ = circle_of(lat)

        def block_of(block, _):
            first = pl.multiple_of(block * 256, 256)
            columns = pl.ds(first, 256)
            result = None
            for trig in (0, 1):
                both = times(left[trig], table[lat, 0, trig, :, columns])
                term = (both[:low_rows] + both[low_rows:]
                        + times(left[trig, :low_rows], table[lat, 1, trig, :, columns]))
                result = term if result is None else result + term
            number = lax.broadcasted_iota(jnp.int32, (16, 256), 1) + first
            for strip in range(STRIPS):
                piece = jnp.where(number + strip * STRIP < whole, result[strip * 16 : strip * 16 + 16], 0.0)
                where = pl.ds(pl.multiple_of(first + strip * STRIP, 256), 256)
                warm_t[lat, :, where] = piece[:8]
                warm_s[lat, :, where] = piece[8:]
            return 0

        lax.fori_loop(0, STRIP // 256, block_of, 0)
        return 0

    for lat in range(2):
        twists(lat)
        tables(lat)
    legendre_sums(1)
    lower = jnp.zeros((64, 128), jnp.float32)
    for duo in range(4):
        lower = lower + depth[2 * duo] * summed[duo, :, :128] + depth[2 * duo + 1] * summed[duo, :, 128:]
    send_c[...] = lower
    lev_copies = []
    for step in range(1, PEERS):
        copy = pltpu.make_async_remote_copy(
            src_ref=send_c, dst_ref=got_c.at[lev],
            send_sem=lev_send.at[step - 1], recv_sem=lev_recv.at[step - 1],
            device_id=(wave, lax.rem(lev + step, PEERS)), device_id_type=MESH)
        copy.start()
        lev_copies.append(copy)
    first = send_fourier(1)
    legendre_sums(0)
    for copy in lev_copies:
        copy.wait_recv()
    above = jnp.zeros((64, 128), jnp.float32)
    got_c[lev] = send_c[...]
    for other in range(PEERS):
        above = above + jnp.where(other > lev, got_c[other], 0.0)
    above = in_order(above)
    for place in range(4):
        send_f[0, pl.ds(32 + place, 16, stride=40), :] = above[16 * place : 16 * place + 16]
    second = send_fourier(0)
    arrived(*first)
    lax.fori_loop(0, 2, warm, 0)
    arrived(*second)
    out_fourier[...] = got_f[...]
    for copy in copies + lev_copies:
        copy.wait_send()
    table_copy(0).wait()
    table_copy(1).wait()


def exchange(pairs, lon_counts, lat_order, depth, spectral, legendre):
    anywhere = pl.BlockSpec(memory_space=pl.ANY)
    vector = pl.BlockSpec(memory_space=pltpu.VMEM)
    scalar = pl.BlockSpec(memory_space=pltpu.SMEM)
    dma = pltpu.SemaphoreType.DMA
    return pl.pallas_call(
        exchange_kernel,
        out_shape=[
            jax.ShapeDtypeStruct((2, PEERS * 40, 128), jnp.float32),
            jax.ShapeDtypeStruct((8, 640), jnp.float32),
            jax.ShapeDtypeStruct((2, 8, LON_PAD), jnp.float32),
            jax.ShapeDtypeStruct((2, 8, LON_PAD), jnp.float32),
            jax.ShapeDtypeStruct((2, 2, 2, WAVES, STRIP), jnp.bfloat16),
        ],
        in_specs=[scalar] * 4 + [anywhere] * 2,
        out_specs=[vector] * 4 + [anywhere],
        scratch_shapes=[
            pltpu.VMEM((6, 648, 640), jnp.bfloat16),
            pltpu.VMEM((SHARE, 32, 1296), jnp.bfloat16),
            *[pltpu.VMEM((2, PEERS, rows, 128), jnp.bfloat16) for rows in THIRDS],
            *[pltpu.VMEM((2, PEERS, rows, 128), jnp.bfloat16) for rows in THIRDS],
            pltpu.VMEM((PEERS * 648, 128), jnp.float32),
            pltpu.VMEM((4, 1296, 256), jnp.bfloat16),
            pltpu.VMEM((SHARE * 64, 1296), jnp.bfloat16),
            pltpu.VMEM((8, 3, 256, 256), jnp.bfloat16),
            pltpu.VMEM((4, 64, 256), jnp.float32),
            pltpu.VMEM((4, 64, 256), jnp.float32),
            pltpu.VMEM((64, 64), jnp.bfloat16),
            pltpu.VMEM((2, PEERS * 40, 128), jnp.float32),
            pltpu.VMEM((2, PEERS * 40, 128), jnp.float32),
            pltpu.VMEM((64, 128), jnp.float32),
            pltpu.VMEM((PEERS, 64, 128), jnp.float32),
            pltpu.VMEM((640, 128), jnp.float32),
            pltpu.VMEM((2, 2, 2, WAVES, STRIP), jnp.bfloat16),
            pltpu.VMEM((3, 8, WAVES), jnp.float32),
            pltpu.VMEM((2, 2, 8, WAVES), jnp.float32),
            pltpu.VMEM((2, STRIPS * 32, WAVES), jnp.bfloat16),
            dma((2,)), dma, dma((2, 3, 15)), dma((2, 3, 15)), dma((2, 3)),
            dma((2, 15)), dma((2, 15)), dma((2,)), dma((15,)), dma((15,)), dma((2,)),
        ],
        compiler_params=pltpu.CompilerParams(
            collective_id=0, has_side_effects=True, vmem_limit_bytes=60 * 2**20
        ),
    )(pairs, lon_counts, lat_order, depth, spectral, legendre)


def synthesis_kernel(lon_counts, lat_order, depth, diagonal, fourier_far, pair_far, warm_t, warm_s, basis,
                     out_v, out_d, out_t, out_s, out_h,
                     table, left, twist, coef, upper, fourier, pair_row, near_t, near_s, table_sem):
    lat = pl.program_id(0)
    wave_group = lax.axis_index("wave")

    def load(which):
        return pltpu.make_async_copy(basis.at[which], table.at[which], table_sem.at[which])

    passed = (pltpu.make_async_copy(warm_t, near_t, table_sem.at[4]),
              pltpu.make_async_copy(warm_s, near_s, table_sem.at[5]))

    @pl.when(lat == 0)
    def _():
        near = (pltpu.make_async_copy(pair_far, pair_row, table_sem.at[2]),
                pltpu.make_async_copy(fourier_far, fourier, table_sem.at[3]))
        for copy in near:
            copy.start()
        load(0).start()
        load(1).start()
        for copy in passed:
            copy.start()
        for copy in near:
            copy.wait()

    circle_whole = lon_counts[lat_order[2 * wave_group + lat]]
    low_rows = STRIPS * 24
    lane = lax.broadcasted_iota(jnp.int32, (1, 128), 1)

    def spread(take, keep, height):
        for place in range(3):
            tiles = [jnp.zeros((height, 128), jnp.float32)] * 5
            for source in range(PEERS):
                value = take(source)
                for side in range(2):
                    goal = source * SHARE + 20 * side
                    tile, offset = goal // 128, goal % 128
                    rolled = pltpu.roll(value, (offset - place * 20 - 64 * side) % 128, 1)
                    end = offset + 20
                    tiles[tile] = jnp.where((lane >= offset) & (lane < end), rolled, tiles[tile])
                    if end > 128:
                        tiles[tile + 1] = jnp.where(lane < end - 128, rolled, tiles[tile + 1])
            for tile in range(5):
                keep(place, tile, tiles[tile])

    def turned(which, _):
        count = lon_counts[lat_order[2 * wave_group + which]]
        circle = jnp.full((1, 1), count, jnp.int32).astype(jnp.float32)
        for part in range(2):
            for side in range(2):
                def take(source, part=part, side=side):
                    return fourier[part, pl.ds(pl.multiple_of(source * 40 + which * 16 + side * 8, 8), 8), :]

                def keep(place, tile, value, part=part, side=side):
                    at = side * 640 + tile * 128
                    coef[3 * part + place, :, at : at + 128] = value

                spread(take, keep, 8)

        def take_above(source):
            return fourier[0, source * 40 + 32 : source * 40 + 36, :]

        def keep_above(place, tile, value):
            upper[place, :, tile * 128 : tile * 128 + 128] = value

        spread(take_above, keep_above, 4)

        pair = pair_row[:1, :]
        wave = jnp.concatenate([pair, TRUNC - pair], axis=1)
        weight = jnp.where(2.0 * wave < circle, jnp.where(wave == 0.0, 1.0, 2.0), 0.0)
        start = (lax.broadcasted_iota(jnp.int32, (8, WAVES), 0) * STRIP).astype(jnp.float32)
        cosine, sine = turn(start * wave, circle)
        twist[0] = cosine * weight
        twist[1] = sine * weight
        level_of = lax.broadcasted_iota(jnp.int32, (8, 1), 0)

        def rows_of(field):
            if field < 2:
                return coef[2 * field], coef[2 * field + 1]
            real, imaginary = coef[4], coef[5]
            higher = []
            for value, place in ((real, 1), (imaginary, 2)):
                total = jnp.broadcast_to(
                    jnp.concatenate([upper[place, pl.ds(2 * which, 1), :], upper[place, pl.ds(2 * which + 1, 1), :]], axis=1),
                    (8, WAVES))
                for level in range(8):
                    share = jnp.where(level_of == level, diagonal[level],
                                      jnp.where(level_of < level, depth[level], 0.0))
                    total = total + share * value[level : level + 1, :]
                higher.append(total)
            return higher[0], higher[1]

        for field in range(3):
            real, imaginary = rows_of(field)
            for strip in range(STRIPS):
                at = strip * 24 + field * 8
                cosine = twist[0, strip : strip + 1, :]
                sine = twist[1, strip : strip + 1, :]
                high, low = halves(real * cosine - imaginary * sine)
                left[which, 0, at : at + 8, :] = high
                left[which, 0, low_rows + at : low_rows + at + 8, :] = low
                high, low = halves(-(real * sine + imaginary * cosine))
                left[which, 1, at : at + 8, :] = high
                left[which, 1, low_rows + at : low_rows + at + 8, :] = low

        return 0

    @pl.when(lat == 0)
    def _():
        lax.fori_loop(0, 2, turned, 0)

    load(lat).wait()

    def block_of(block, _):
        first = pl.multiple_of(block * 256, 256)
        columns = pl.ds(first, 256)
        times = functools.partial(jnp.dot, preferred_element_type=jnp.float32)
        result = None
        for trig in (0, 1):
            high = table[lat, 0, trig, :, columns]
            both = times(left[lat, trig], high)
            term = (both[:low_rows] + both[low_rows:]
                    + times(left[lat, trig, :low_rows], table[lat, 1, trig, :, columns]))
            result = term if result is None else result + term
        number = lax.broadcasted_iota(jnp.int32, (24, 256), 1) + first
        for strip in range(STRIPS):
            piece = jnp.where(number + strip * STRIP < circle_whole,
                              result[strip * 24 : strip * 24 + 24], 0.0)
            where = pl.ds(pl.multiple_of(first + strip * STRIP, 256), 256)
            for field, out in enumerate((out_v, out_d, out_h)):
                out[0, :, where] = piece[field * 8 : field * 8 + 8]
        return 0

    lax.fori_loop(0, STRIP // 256, block_of, 0)

    @pl.when(lat == 0)
    def _():
        for copy in passed:
            copy.wait()

    out_t[0] = near_t[lat]
    out_s[0] = near_s[lat]


def synthesize(lon_counts, lat_order, depth, diagonal, fourier, pair_row, warm_t, warm_s, basis):
    anywhere = pl.BlockSpec(memory_space=pl.ANY)
    scalar = pl.BlockSpec(memory_space=pltpu.SMEM)
    grid_line = pl.BlockSpec((1, 8, LON_PAD), lambda i: (i, 0, 0))
    return pl.pallas_call(
        synthesis_kernel,
        grid=(2,),
        out_shape=[jax.ShapeDtypeStruct((2, 8, LON_PAD), jnp.float32)] * 5,
        in_specs=[scalar] * 4 + [anywhere] * 5,
        out_specs=[grid_line] * 5,
        scratch_shapes=[
            pltpu.VMEM((2, 2, 2, WAVES, STRIP), jnp.bfloat16),
            pltpu.VMEM((2, 2, STRIPS * 48, WAVES), jnp.bfloat16),
            pltpu.VMEM((2, 8, WAVES), jnp.float32),
            pltpu.VMEM((6, 8, WAVES), jnp.float32),
            pltpu.VMEM((3, 4, 640), jnp.float32),
            pltpu.VMEM((2, PEERS * 40, 128), jnp.float32),
            pltpu.VMEM((8, 640), jnp.float32),
            pltpu.VMEM((2, 8, LON_PAD), jnp.float32),
            pltpu.VMEM((2, 8, LON_PAD), jnp.float32),
            pltpu.SemaphoreType.DMA((6,)),
        ],
        compiler_params=pltpu.CompilerParams(vmem_limit_bytes=60 * 2**20),
    )(lon_counts, lat_order, depth, diagonal, fourier, pair_row, warm_t, warm_s, basis)


def body(
    spectral, legendre, pair_list, lon_counts, lat_order, layer_depth_log, diagonal_layer_factor
):
    rows = jnp.transpose(spectral, (0, 2, 1, 3)).reshape(6, 648, 640)
    polynomials = jnp.transpose(legendre, (0, 2, 1))
    fourier, pair_row, warm_t, warm_s, basis = exchange(
        pair_list, lon_counts, lat_order, layer_depth_log, rows, polynomials
    )
    return tuple(
        synthesize(lon_counts, lat_order, layer_depth_log, diagonal_layer_factor, fourier, pair_row,
                   warm_t, warm_s, basis)
    )


def solution(mesh):
    placed = (
        P(None, "lev", "wave", None),
        P("wave", None, None),
        P(),
        P(),
        P(),
        P("lev"),
        P("lev"),
    )
    return jax.shard_map(
        body,
        mesh=mesh,
        in_specs=placed,
        out_specs=(P("wave", "lev", None),) * 5,
        check_vma=False,
    )
```
